256 devices in a mesh: section: 16 (over x, y), expert: 16 (over z, core).
Axes of the slice: x: 4, y: 4, z: 8, core: 2. Of those that a mesh axis runs over, the one named last changes fastest.
Arguments:
- tokens: bfloat16 [16, 256, 7168], P('section', 'expert'), may hold values from -6 to 6
- norm_gain: float32 [16, 7168], P('section'), may hold values from 0.1 to 1.9
- gate_weight: bfloat16 [16, 7168, 4096], P('section', None, 'expert'), may hold values from -0.0625 to 0.0625
- up_weight: bfloat16 [16, 7168, 4096], P('section', None, 'expert'), may hold values from -0.0625 to 0.0625
- down_weight: bfloat16 [16, 4096, 7168], P('section', 'expert'), may hold values from -0.1875 to 0.1875
- block_scales: int32 [16, 3, 56, 32], P('section', None, None, 'expert'), may hold values from -1 to 1
- routes: int32 [16, 2, 256, 2], P('section', None, 'expert'), may hold values from 0 to 3, all different within a row; in each aligned block of 16 rows (0 to 15, 16 to 31, ..., all dimensions but the last counted through in order) at most 12 rows name the same one
- route_weights: bfloat16 [16, 2, 256, 2], P('section', None, 'expert'), may hold values from 0.19921875 to 1
Outputs:
- final: bfloat16 [16, 256, 7168], P('section', 'expert')
The draws below stay inside these ranges and needn't reach their ends.
Inputs may be any that keep to these rules, and one draw needn't show every extreme that they name: `routes`: each token names 2 different experts. For each section and step, the 16 tokens of one device name no expert more than 12 times.
All inputs are finite; a program needn't handle non-finite values.
Results may differ from the reference program's by a relative error of at most 0.025.
Values may be sent and summed in bfloat16 or wider, within the bound.
No kernel may reach another device: no remote copies, remote signals or barrier semaphores. Data moves between devices by JAX's collectives and lax.ppermute only.
A program may use at most 128 MiB of HBM per device.

```python
import math
import jax
import jax.numpy as jnp
import numpy as np
from jax import lax

D = 7168
FE = 1024
SPLIT = 4
TOPK = 2
TICKS = 2
TOK_DEV = 16
EXPERTS = 4
MB_ROWS = 256
CAP = 12
N_SECTION = 16
N_EXPERT = 16


def set_ends(entries, key, smallest, top_value):
    dims = entries.shape
    place = [jax.random.randint(jax.random.fold_in(key, axis), (), 0, dims[axis]) for axis in range(len(dims))]
    entries = entries.at[tuple(place)].set(smallest)
    longest = dims.index(max(dims))
    place[longest] = (place[longest] + 1) % dims[longest]
    return entries.at[tuple(place)].set(top_value)


def level_of(own_key, extent, cuts, least, high):
    gain = 1.0
    for axis_at, blocks in cuts:
        steps = jax.random.uniform(jax.random.fold_in(jax.random.fold_in(own_key, 6), axis_at), (blocks,), jnp.float32, least / len(cuts), high / len(cuts))
        gain = gain * jnp.repeat(jnp.exp(steps), extent[axis_at] // blocks).reshape((-1,) + (1,) * (len(extent) - 1 - axis_at))
    return gain


def assign_block(key, own, number, rows, amount, top, limit, slope):
    order = jax.random.permutation(key, amount)
    heavy_load, usual = portions_of(amount, rows * top, limit, slope, True), portions_of(amount, rows * top, limit, slope, False)
    places = jnp.arange(amount)

    def named(tallies, rotation):
        used = int((tallies > 0).sum())
        fixed = max(1, used // 4)
        passed = fixed + (places - fixed + rotation * (used - fixed)) % max(1, amount - fixed)
        return jnp.zeros((amount,), jnp.int32).at[order[jnp.where(places < fixed, places, passed)]].set(jnp.asarray(tallies, jnp.int32))

    tallies = jnp.where(number % 4 == 0, named(heavy_load, number // 4), named(usual, number - number // 4 - 1))
    mixed = jax.random.permutation(jax.random.fold_in(own, 3), amount)
    source_of, sink = mixed[0:amount // 2 * 2:2], mixed[1:amount // 2 * 2:2]
    room = jnp.minimum(tallies[source_of] - 1, limit - tallies[sink]) // 2
    room = jnp.where((source_of == order[0]) | (sink == order[0]) | (tallies[sink] == 0), 0, jnp.maximum(room, 0))
    passed = jax.random.randint(jax.random.fold_in(own, 4), (amount // 2,), 0, 1 << 20) % (room + 1)
    tallies = tallies.at[source_of].add(-passed).at[sink].add(passed)
    items = jnp.searchsorted(jnp.cumsum(tallies), jnp.arange(rows * top), side="right").astype(jnp.int32)
    grid = items.reshape(top, rows).T
    grid = grid[jax.random.permutation(jax.random.fold_in(own, 1), rows)]
    rotation = jax.random.randint(jax.random.fold_in(own, 2), (rows, 1), 0, top)
    return jnp.take_along_axis(grid, (jnp.arange(top)[None, :] + rotation) % top, axis=1)


def portions_of(amount, total, most, lean, full):
    loads = [(1 << 20) // math.isqrt(grade ** lean) + 1 for grade in range(1, amount + 1)]
    largest = most if full else min(most, max(-(-total // amount), total * loads[0] // sum(loads)))
    least = 1 if total - largest >= amount - 1 else 0
    holding, rest = [largest] + [least] * (amount - 1), total - largest - least * (amount - 1)
    while rest > 0:
        movable = [i for i in range(1, amount) if holding[i] < largest] or [i for i in range(1, amount) if holding[i] < most]
        whole, budget = sum([loads[i] for i in movable]), rest
        for i in movable:
            extra = min(most - holding[i], max(1, budget * loads[i] // whole), rest)
            holding[i] = holding[i] + extra
            rest = rest - extra
    return np.array(holding)


def bell_draw(stream_key, shape, scale, reach, cuts=(), held_as=jnp.bfloat16):
    array = jax.random.normal(stream_key, shape, jnp.float32) * scale
    if len(cuts) > 0:
        array = level_of(stream_key, shape, cuts, -0.22, 0.18) * array
    return jnp.clip(array, min=-reach, max=reach).astype(held_as)


def setup_inputs(seed: int = 0) -> dict:
    seeds = jax.random.split(jax.random.key(seed), 9)
    tokens = bell_draw(seeds[0], (N_SECTION, MB_ROWS, D), 1.0, 6.0, ((0, 16), (1, 16)))
    norm_gain = jnp.clip(1.0 + 0.18 * jax.random.normal(seeds[1], (N_SECTION, D), jnp.float32), 0.1, 1.9)
    gate_weight = bell_draw(seeds[2], (N_SECTION, D, EXPERTS * FE), D ** -0.5, 0.0625, ((0, 16), (2, 16)))
    up_weight = bell_draw(seeds[3], (N_SECTION, D, EXPERTS * FE), D ** -0.5, 0.0625, ((0, 16), (2, 16)))
    down_weight = bell_draw(seeds[4], (N_SECTION, EXPERTS * FE, D), FE ** -0.5, 0.1875, ((0, 16), (1, 16)))
    block_scales = set_ends(jax.random.randint(seeds[5], (N_SECTION, 3, D // 128, EXPERTS * FE // 128), -1, 2), jax.random.fold_in(seeds[5], 1), -1, 1).astype(jnp.int32)
    routes_keys = jax.random.split(jax.random.fold_in(seeds[6], 1), N_SECTION * TICKS * MB_ROWS // TOK_DEV)
    routes_turns = jax.random.permutation(jax.random.fold_in(seeds[6], 3), N_SECTION * TICKS * MB_ROWS // TOK_DEV)
    routes = jax.vmap(lambda own, number: assign_block(jax.random.fold_in(seeds[6], 2), own, number, TOK_DEV, EXPERTS, TOPK, CAP, 2))(routes_keys, routes_turns).reshape((N_SECTION, TICKS, MB_ROWS, TOPK))
    route_weights = jnp.clip(0.19921875 + 0.80078125 * jax.random.uniform(seeds[7], (N_SECTION, TICKS, MB_ROWS, TOPK), jnp.float32) ** level_of(seeds[7], (N_SECTION, TICKS, MB_ROWS, TOPK), ((0, 16), (2, 16)), -0.2, 0.2), 0.19921875, 1.0).astype(jnp.bfloat16)
    return {"tokens": tokens, "norm_gain": norm_gain, "gate_weight": gate_weight, "up_weight": up_weight, "down_weight": down_weight, "block_scales": block_scales, "routes": routes, "route_weights": route_weights}


def dequantize(stored, exponents):
    height, span_cols = stored.shape
    factor = jnp.exp2(exponents.astype(jnp.float32))
    blocked = stored.reshape(height // 128, 128, span_cols // 128, 128).astype(jnp.float32)
    return (blocked * factor[:, None, :, None]).reshape(height, span_cols).astype(jnp.bfloat16)

def rms_normed(current, norm_gain):
    values = current.astype(jnp.float32)
    mean_sq = lax.optimization_barrier(jnp.mean(values * values, axis=-1, keepdims=True))
    return (values * lax.rsqrt(mean_sq + 1e-06) * norm_gain).astype(jnp.bfloat16)

def one_layer(operands):
    current, norm_gain, gate_weight, up_weight, down_weight, block_scales, routes, route_weights = operands
    hidden_dev = FE // SPLIT
    gate_full = dequantize(gate_weight, block_scales[0])
    up_full = dequantize(up_weight, block_scales[1])
    down_full = dequantize(down_weight, block_scales[2].T)
    normed = rms_normed(current, norm_gain)
    expert_ids = jnp.arange(EXPERTS, dtype=jnp.int32)
    matches = (routes[:, :, None] == expert_ids[None, None, :]).astype(jnp.float32)
    token_weight = lax.optimization_barrier(jnp.sum(matches * route_weights.astype(jnp.float32)[:, :, None], axis=1))
    per_block = jnp.repeat(token_weight.T, SPLIT, axis=0)
    gate_blocks = gate_full.reshape(D, N_EXPERT, hidden_dev).transpose(1, 0, 2)
    up_blocks = up_full.reshape(D, N_EXPERT, hidden_dev).transpose(1, 0, 2)
    down_blocks = down_full.reshape(N_EXPERT, hidden_dev, D)

    def add_block(summed, pieces):
        gate_piece, up_piece, down_piece, weight_piece = pieces
        gate_out = jnp.dot(normed, gate_piece, preferred_element_type=jnp.float32)
        up_out = jnp.dot(normed, up_piece, preferred_element_type=jnp.float32)
        hidden = (jax.nn.silu(gate_out) * up_out).astype(jnp.bfloat16)
        product = jnp.dot(hidden, down_piece, preferred_element_type=jnp.float32)
        partial_out = (product * weight_piece[:, None]).astype(jnp.bfloat16)
        return (summed + partial_out.astype(jnp.float32), None)
    start_sum = jnp.zeros((current.shape[0], D), jnp.float32)
    summed, unused = lax.scan(add_block, start_sum, (gate_blocks, up_blocks, down_blocks, per_block))
    return (current.astype(jnp.float32) + summed).astype(jnp.bfloat16)

def reference(tokens, norm_gain, gate_weight, up_weight, down_weight, block_scales, routes, route_weights):
    current = tokens
    for tick_index in range(TICKS):
        current = lax.map(one_layer, (current, norm_gain, gate_weight, up_weight, down_weight, block_scales, routes[:, tick_index], route_weights[:, tick_index]))
        current = jnp.roll(current, 1, axis=0)
    return current
```

```python
import jax
import jax.numpy as jnp
from jax import lax
from jax.experimental import pallas as pl
from jax.experimental.pallas import tpu as pltpu
from jax.sharding import PartitionSpec as P

SPLIT = 4
TICKS = 2
LANES = 128
VMEM_LIMIT = 44 * 1024 * 1024
F32 = jnp.float32
BF16 = jnp.bfloat16


def along_z(shard, by):
    length = lax.axis_size("expert")
    return lax.ppermute(
        shard, "expert", [(i, (i + 2 * by) % length) for i in range(length)]
    )


def other_core(shard):
    length = lax.axis_size("expert")
    return lax.ppermute(shard, "expert", [(i, i ^ 1) for i in range(length)])


def next_section(shard):
    length = lax.axis_size("section")
    return lax.ppermute(shard, "section", [(i, (i + 1) % length) for i in range(length)])


def cut_of(width):
    return width // LANES // 2 * LANES


def gather_first(block):
    far_back, far_ahead = along_z(block, 2), along_z(block, -2)
    return [block, along_z(block, 1), along_z(block, -1), far_back, far_ahead]


def gather_second(first):
    far_back, far_ahead = first[3], first[4]
    cut = cut_of(far_back.shape[1])
    return first + [
        along_z(far_back, 1),
        along_z(far_ahead, -1),
        along_z(far_back[:, :cut], 2),
        along_z(far_ahead[:, cut:], -2),
    ]


def sum_first(outs):
    arrived = [
        along_z(outs[5], -1),
        along_z(outs[6], 1),
        along_z(outs[7], -2),
        along_z(outs[8], 2),
    ]
    near = [along_z(outs[1], -1), along_z(outs[2], 1)]
    return outs, arrived, near


def join_far(outs, arrived):
    rows, width = outs[3].shape
    cut = cut_of(width)

    def kernel(back, ahead, b3, a3, left, right, back_out, ahead_out):
        lo, hi = slice(0, cut), slice(cut, width)
        f = lambda ref, cols: ref[:, cols].astype(F32)
        back_out[:, lo] = (f(back, lo) + f(b3, lo) + left[...].astype(F32)).astype(BF16)
        back_out[:, hi] = (f(back, hi) + f(b3, hi)).astype(BF16)
        ahead_out[:, lo] = (f(ahead, lo) + f(a3, lo)).astype(BF16)
        ahead_out[:, hi] = (f(ahead, hi) + f(a3, hi) + right[...].astype(F32)).astype(BF16)

    shape = jax.ShapeDtypeStruct((rows, width), BF16)
    return pl.pallas_call(
        kernel,
        out_shape=[shape, shape],
        compiler_params=pltpu.CompilerParams(vmem_limit_bytes=VMEM_LIMIT),
        cost_estimate=pl.CostEstimate(
            flops=6 * rows * width, bytes_accessed=14 * rows * width, transcendentals=0
        ),
        name="join_far",
    )(outs[3], outs[4], *arrived)


def sum_second(parts):
    outs, arrived, near = parts
    back, ahead = join_far(outs, arrived)
    return [outs[0], *near, along_z(back, -2), along_z(ahead, 2)]


def total(state, parts):
    value = state.astype(F32)
    for part in parts:
        value = value + part.astype(F32)
    return value.astype(BF16)


def load_rows(pieces, gain, rows_ref, squares_ref):
    height = pieces[0].shape[0]
    width = gain.shape[1]
    cut = cut_of(pieces[0].shape[1])

    def put(ref, at, lo, hi, base):
        held = None
        for c in range(lo, hi, LANES):
            x = ref[:, c - base : c - base + LANES].astype(F32)
            held = x * x if held is None else held + x * x
            rows_ref[at : at + height, c : c + LANES] = (
                x * gain[:, c : c + LANES]
            ).astype(BF16)
        return held

    for n in range(8):
        at = n * height
        if n < 7:
            held = put(pieces[n], at, 0, width, 0)
        else:
            held = put(pieces[7], at, 0, cut, 0) + put(pieces[8], at, cut, width, cut)
        squares_ref[at : at + height, :] = held


def load_table(pieces, width, table_ref):
    height = pieces[0].shape[0]
    cut = cut_of(pieces[0].shape[1])
    for n in range(8):
        ref, lo = (pieces[n], width) if n < 7 else (pieces[8], width - cut)
        table_ref[n * height : (n + 1) * height, :] = ref[:, lo : lo + LANES].astype(F32)


def scaled(block, factor):
    return block * jnp.full(block.shape, factor, F32).astype(BF16)


def experts_share(pieces, gain, weights, factors, table, own_lane):
    width = gain.shape[1]
    hidden_width = weights[0][0].shape[1]
    height = pieces[0].shape[0]
    rows = 8 * height
    blocks, halves = width // LANES, hidden_width // LANES
    per_tile = 8 if blocks % 8 == 0 else 4
    tile = per_tile * LANES
    cut = cut_of(width)
    n_pieces = len(pieces)
    new_table = table is None

    def kernel(*refs):
        lane_ref, factor_refs, ins = refs[0], refs[1:3], refs[3 : 3 + n_pieces]
        gain_ref, rest = refs[3 + n_pieces], refs[4 + n_pieces :]
        gates, ups, downs, rest = rest[0:2], rest[2:4], rest[4:6], rest[6:]
        if not new_table:
            table_in, rest = rest[0], rest[1:]
        outs, table_ref = rest[:9], rest[9]
        rows_ref, tile_ref, down_ref, acc_ref, squares_ref, hidden_ref, weight_ref = rest[10:]

        load_rows(ins, gain_ref, rows_ref, squares_ref)
        if new_table:
            load_table(ins, width, table_ref)
        else:
            table_ref[...] = table_in[...]

        def add_tile(step, first):
            start = pl.multiple_of(step * tile, LANES)
            for which, pair in enumerate((gates, ups)):
                for core in range(2):
                    for a in range(per_tile):
                        for b in range(halves):
                            at = (which * blocks + step * per_tile + a) * halves + b
                            block = pair[core][
                                pl.ds(pl.multiple_of(start + a * LANES, LANES), LANES),
                                b * LANES : (b + 1) * LANES,
                            ]
                            column = (which * 2 + core) * hidden_width + b * LANES
                            tile_ref[
                                a * LANES : (a + 1) * LANES, column : column + LANES
                            ] = scaled(block, factor_refs[core][at])
            product = jnp.dot(
                rows_ref[:, pl.ds(start, tile)], tile_ref[...], preferred_element_type=F32
            )
            acc_ref[...] = product if first else acc_ref[...] + product

        add_tile(0, True)
        lax.fori_loop(1, width // tile, lambda i, c: (add_tile(i, False), c)[1], 0)

        mean = jnp.sum(squares_ref[...], axis=-1, keepdims=True) / width
        factor = lax.rsqrt(mean + 1e-06)
        gate = acc_ref[:, : 2 * hidden_width] * factor
        up = acc_ref[:, 2 * hidden_width :] * factor
        hidden_ref[...] = (gate / (1.0 + jnp.exp(-gate)) * up).astype(BF16)
        lane = lax.broadcasted_iota(jnp.int32, (rows, LANES), 1)
        picked = jnp.where(lane == lane_ref[0], table_ref[...], 0.0)
        weight_ref[...] = jnp.broadcast_to(
            jnp.sum(picked, axis=-1, keepdims=True), (rows, LANES)
        )

        for step in range(width // tile):
            for core in range(2):
                for a in range(per_tile):
                    for b in range(halves):
                        at = (2 * blocks + step * per_tile + a) * halves + b
                        lo = step * tile + a * LANES
                        block = downs[core][b * LANES : (b + 1) * LANES, lo : lo + LANES]
                        row = core * hidden_width + b * LANES
                        down_ref[row : row + LANES, a * LANES : (a + 1) * LANES] = scaled(
                            block, factor_refs[core][at]
                        )
            product = jnp.dot(hidden_ref[...], down_ref[...], preferred_element_type=F32)
            product = (product * weight_ref[:, :1]).astype(BF16)
            lo, hi = step * tile, (step + 1) * tile
            for n in range(7):
                outs[n][:, lo:hi] = product[n * height : (n + 1) * height, :]
            last = product[7 * height :, :]
            if lo < cut:
                outs[7][:, lo : min(hi, cut)] = last[:, : min(hi, cut) - lo]
            if hi > cut:
                outs[8][:, max(lo, cut) - cut : hi - cut] = last[:, max(lo, cut) - lo :]

    smem, vmem = pl.BlockSpec(memory_space=pltpu.SMEM), pl.BlockSpec(memory_space=pltpu.VMEM)
    tables = [] if new_table else [table]
    operands = [*pieces, gain, *weights[0], *weights[1], *weights[2], *tables]
    out_sizes = [(height, width)] * 7 + [(height, cut), (height, width - cut)]
    results = pl.pallas_call(
        kernel,
        in_specs=[smem] * 3 + [vmem] * len(operands),
        out_specs=[vmem] * 10,
        out_shape=[jax.ShapeDtypeStruct(s, BF16) for s in out_sizes]
        + [jax.ShapeDtypeStruct((rows, LANES), F32)],
        scratch_shapes=[
            pltpu.VMEM((rows, width), BF16),
            pltpu.VMEM((tile, 4 * hidden_width), BF16),
            pltpu.VMEM((2 * hidden_width, tile), BF16),
            pltpu.VMEM((rows, 4 * hidden_width), F32),
            pltpu.VMEM((rows, LANES), F32),
            pltpu.VMEM((rows, 2 * hidden_width), BF16),
            pltpu.VMEM((rows, LANES), F32),
        ],
        compiler_params=pltpu.CompilerParams(vmem_limit_bytes=VMEM_LIMIT),
        cost_estimate=pl.CostEstimate(
            flops=12 * rows * width * hidden_width,
            bytes_accessed=12 * width * hidden_width,
            transcendentals=2 * rows * hidden_width,
        ),
        name="experts_share",
    )(own_lane, *factors, *operands)
    return results[:9], results[9]


def weights_table(routes, route_weights, experts):
    ids = jnp.arange(experts, dtype=jnp.int32)
    matches = (routes[..., None] == ids).astype(F32)
    table = jnp.sum(matches * route_weights.astype(F32)[..., None], axis=2)
    table = table.transpose(1, 0, 2).reshape(table.shape[1], TICKS * experts)
    return jnp.pad(table, ((0, 0), (0, LANES - TICKS * experts))).astype(BF16)


def per_device(
    tokens, norm_gain, gate_weight, up_weight, down_weight, block_scales, routes, route_weights
):
    experts = lax.axis_size("expert") // SPLIT
    own_expert = lax.axis_index("expert") // SPLIT
    factors = jnp.exp2(block_scales[0].astype(F32)).reshape(-1)
    factors = (factors, other_core(factors))
    weights = [(w[0], other_core(w[0])) for w in (gate_weight, up_weight, down_weight)]

    state = tokens[0]
    table = weights_table(routes[0], route_weights[0], experts)
    held_table = None
    for tick in range(TICKS):
        rows = state if tick else jnp.concatenate([state, table], axis=1)
        pieces = gather_second(gather_first(rows))
        own_lane = (own_expert + tick * experts).astype(jnp.int32).reshape(1)
        outs, held_table = experts_share(
            pieces, norm_gain, weights, factors, held_table, own_lane
        )
        state = next_section(total(state, sum_second(sum_first(outs))))
    return state[None]


def solution(mesh):
    in_specs = (
        P("section", "expert", None),
        P("section", None),
        P("section", None, "expert"),
        P("section", None, "expert"),
        P("section", "expert", None),
        P("section", None, None, "expert"),
        P("section", None, "expert", None),
        P("section", None, "expert", None),
    )
    out_specs = P("section", "expert", None)
    return jax.shard_map(
        per_device, mesh=mesh, in_specs=in_specs, out_specs=out_specs, check_vma=False
    )
```

```python
import jax
import jax.numpy as jnp
from jax import lax
from jax.experimental import pallas as pl
from jax.experimental.pallas import tpu as pltpu
from jax.sharding import PartitionSpec as P

SPLIT = 4
TICKS = 2
LANES = 128
VMEM_LIMIT = 16 * 1024 * 1024
AHEAD = 4
F32 = jnp.float32
BF16 = jnp.bfloat16


def along_z(shard, by):
    length = lax.axis_size("expert")
    return lax.ppermute(
        shard, "expert", [(i, (i + 2 * by) % length) for i in range(length)]
    )


def other_core(shard):
    length = lax.axis_size("expert")
    return lax.ppermute(shard, "expert", [(i, i ^ 1) for i in range(length)])


def to_next_section(shard, by):
    sections, length = lax.axis_size("section"), lax.axis_size("expert")
    pairs = [
        (s * length + e, (s + 1) % sections * length + (e + 2 * by) % length)
        for s in range(sections)
        for e in range(length)
    ]
    return lax.ppermute(shard, ("section", "expert"), pairs)


def cut_of(width):
    return width // LANES // 2 * LANES


def gather_first(block):
    far_back, far_ahead = along_z(block, 2), along_z(block, -2)
    return [block, along_z(block, 1), along_z(block, -1), far_back, far_ahead]


def gather_second(first):
    far_back, far_ahead = first[3], first[4]
    cut = cut_of(far_back.shape[1])
    return first + [
        along_z(far_back, 1),
        along_z(far_ahead, -1),
        along_z(far_back[:, :cut], 2),
        along_z(far_ahead[:, cut:], -2),
    ]


def sum_to_next(state, outs):
    arrived = [
        along_z(outs[5], -1),
        along_z(outs[6], 1),
        along_z(outs[7], -2),
        along_z(outs[8], 2),
        along_z(outs[1], -1),
        along_z(outs[2], 1),
    ]
    here, back, ahead = join(state, outs, arrived)
    parts = [to_next_section(back, -2), to_next_section(ahead, 2), to_next_section(here, 0)]
    return sum(part.astype(F32) for part in parts).astype(BF16)


def join(state, outs, arrived):
    rows, width = state.shape
    cut = cut_of(width)

    def kernel(state, near, back, ahead, b3, a3, left, right, b1, a1, here_out, back_out, ahead_out):
        lo, hi = slice(0, cut), slice(cut, width)
        f = lambda ref, cols: ref[:, cols].astype(F32)
        back_out[:, lo] = (f(back, lo) + f(b3, lo) + left[...].astype(F32)).astype(BF16)
        back_out[:, hi] = (f(back, hi) + f(b3, hi)).astype(BF16)
        ahead_out[:, lo] = (f(ahead, lo) + f(a3, lo)).astype(BF16)
        ahead_out[:, hi] = (f(ahead, hi) + f(a3, hi) + right[...].astype(F32)).astype(BF16)
        every = slice(0, width)
        here = f(state, every) + (f(near, every) + f(b1, every) + f(a1, every))
        here_out[...] = here.astype(BF16)

    shape = jax.ShapeDtypeStruct((rows, width), BF16)
    return pl.pallas_call(
        kernel,
        out_shape=[shape] * 3,
        compiler_params=pltpu.CompilerParams(vmem_limit_bytes=VMEM_LIMIT),
        cost_estimate=pl.CostEstimate(
            flops=9 * rows * width, bytes_accessed=24 * rows * width, transcendentals=0
        ),
        name="join",
    )(state, outs[0], outs[3], outs[4], *arrived)


def load_rows(pieces, gain, rows_ref, squares_ref):
    height = pieces[0].shape[0]
    width = gain.shape[1]
    cut = cut_of(pieces[0].shape[1])

    def put(ref, at, lo, hi, base):
        held = None
        for c in range(lo, hi, LANES):
            x = ref[:, c - base : c - base + LANES].astype(F32)
            held = x * x if held is None else held + x * x
            rows_ref[at : at + height, c : c + LANES] = (
                x * gain[:, c : c + LANES]
            ).astype(BF16)
        return held

    for n in range(8):
        at = n * height
        if n < 7:
            held = put(pieces[n], at, 0, width, 0)
        else:
            held = put(pieces[7], at, 0, cut, 0) + put(pieces[8], at, cut, width, cut)
        squares_ref[at : at + height, :] = held


def load_table(pieces, width, table_ref):
    height = pieces[0].shape[0]
    cut = cut_of(pieces[0].shape[1])
    for n in range(8):
        ref, lo = (pieces[n], width) if n < 7 else (pieces[8], width - cut)
        table_ref[n * height : (n + 1) * height, :] = ref[:, lo : lo + LANES].astype(F32)


def scaled(block, factor):
    return block * jnp.full(block.shape, factor, F32).astype(BF16)


def scaled_weights(gate, up, down, factors):
    width, side = gate.shape
    per_block, blocks = side // LANES, width // side
    group = max(n for n in (1, 2, 4) if blocks % n == 0)
    groups = blocks // group

    def kernel(f_ref, gate_ref, up_ref, down_ref, out_ref, sems):
        def copies(n):
            which, at = n // groups, n % groups * group
            if which < 2:
                src = (gate_ref, up_ref)[which].at[pl.ds(at * side, group * side), :]
                dst = out_ref.at[pl.ds(which * width + at * side, group * side), :]
                return [pltpu.make_async_copy(src, dst, sems.at[which, at])]
            return [
                pltpu.make_async_copy(
                    down_ref.at[:, pl.ds(j * side, side)],
                    out_ref.at[pl.ds(2 * width + j * side, side), :],
                    sems.at[which, j],
                )
                for j in range(at, at + group)
            ]

        def scale(n):
            which, at = n // groups, n % groups * group
            for j in range(at, at + group):
                for a in range(per_block):
                    for b in range(per_block):
                        wide, deep = (j * per_block + a, b) if which < 2 else (j * per_block + b, a)
                        factor = f_ref[(which * (width // LANES) + wide) * per_block + deep]
                        row = which * width + j * side + a * LANES
                        place = (slice(row, row + LANES), slice(b * LANES, (b + 1) * LANES))
                        out_ref[place] = scaled(out_ref[place], factor)

        for n in range(3 * groups + AHEAD):
            if n < 3 * groups:
                for copy in copies(n):
                    copy.start()
            if n >= AHEAD:
                for copy in copies(n - AHEAD):
                    copy.wait()
                scale(n - AHEAD)

    return pl.pallas_call(
        kernel,
        in_specs=[pl.BlockSpec(memory_space=pltpu.SMEM)]
        + [pl.BlockSpec(memory_space=pltpu.HBM)] * 3,
        out_specs=pl.BlockSpec(memory_space=pltpu.VMEM),
        out_shape=jax.ShapeDtypeStruct((3 * width, side), BF16),
        scratch_shapes=[pltpu.SemaphoreType.DMA((3, blocks))],
        compiler_params=pltpu.CompilerParams(vmem_limit_bytes=VMEM_LIMIT),
        cost_estimate=pl.CostEstimate(
            flops=3 * width * side, bytes_accessed=12 * width * side, transcendentals=0
        ),
        name="scaled_weights",
    )(factors, gate, up, down)


def experts_share(pieces, gain, weights, table, first_lane):
    width = gain.shape[1]
    side = weights[0].shape[1]
    height = pieces[0].shape[0]
    rows = 8 * height
    cut = cut_of(width)
    tile = side * max(n for n in (1, 2, 4) if width // side % n == 0)
    n_pieces = len(pieces)
    new_table = table is None

    def kernel(*refs):
        ins, gain_ref, own_ref, other_ref = refs[:n_pieces], *refs[n_pieces : n_pieces + 3]
        rest = refs[n_pieces + 3 :]
        if not new_table:
            table_in, rest = rest[0], rest[1:]
        outs, table_ref = rest[:9], rest[9]
        rows_ref, squares_ref, hidden_ref = rest[10:]

        load_rows(ins, gain_ref, rows_ref, squares_ref)
        if new_table:
            load_table(ins, width, table_ref)
        else:
            table_ref[...] = table_in[...]
        mean = jnp.sum(squares_ref[...], axis=-1, keepdims=True) / width
        factor = lax.rsqrt(mean + 1e-06)
        lane = lax.broadcasted_iota(jnp.int32, (rows, LANES), 1)
        own_lane = first_lane + lax.div(lax.axis_index("expert"), SPLIT)
        picked = jnp.where(lane == own_lane, table_ref[...], 0.0)
        weight = jnp.sum(picked, axis=-1, keepdims=True)

        for core, ref in enumerate((own_ref, other_ref)):
            gate = jnp.dot(rows_ref[...], ref[:width, :], preferred_element_type=F32)
            up = jnp.dot(rows_ref[...], ref[width : 2 * width, :], preferred_element_type=F32)
            gate, up = gate * factor, up * factor
            hidden_ref[:, core * side : (core + 1) * side] = (
                gate / (1.0 + jnp.exp(-gate)) * up
            ).astype(BF16)

        for lo in range(0, width, side):
            at = 2 * width + lo
            product = jnp.dot(
                hidden_ref[:, :side], own_ref[at : at + side, :], preferred_element_type=F32
            ) + jnp.dot(
                hidden_ref[:, side:], other_ref[at : at + side, :], preferred_element_type=F32
            )
            product = (product * weight).astype(BF16)
            hi = lo + side
            for n in range(7):
                outs[n][:, lo:hi] = product[n * height : (n + 1) * height, :]
            last = product[7 * height :, :]
            if lo < cut:
                outs[7][:, lo : min(hi, cut)] = last[:, : min(hi, cut) - lo]
            if hi > cut:
                outs[8][:, max(lo, cut) - cut : hi - cut] = last[:, max(lo, cut) - lo :]

    vmem = pl.BlockSpec(memory_space=pltpu.VMEM)
    tables = [] if new_table else [table]
    operands = [*pieces, gain, *weights, *tables]
    out_sizes = [(height, width)] * 7 + [(height, cut), (height, width - cut)]
    results = pl.pallas_call(
        kernel,
        in_specs=[vmem] * len(operands),
        out_specs=[vmem] * 10,
        out_shape=[jax.ShapeDtypeStruct(s, BF16) for s in out_sizes]
        + [jax.ShapeDtypeStruct((rows, LANES), F32)],
        scratch_shapes=[
            pltpu.VMEM((rows, width), BF16),
            pltpu.VMEM((rows, LANES), F32),
            pltpu.VMEM((rows, 2 * side), BF16),
        ],
        compiler_params=pltpu.CompilerParams(vmem_limit_bytes=VMEM_LIMIT),
        cost_estimate=pl.CostEstimate(
            flops=12 * rows * width * side,
            bytes_accessed=12 * width * side,
            transcendentals=2 * rows * side,
        ),
        name="experts_share",
    )(*operands)
    return results[:9], results[9]


def weights_table(routes, route_weights, experts):
    ids = jnp.arange(experts, dtype=jnp.int32)
    matches = (routes[..., None] == ids).astype(F32)
    table = jnp.sum(matches * route_weights.astype(F32)[..., None], axis=2)
    table = table.transpose(1, 0, 2).reshape(table.shape[1], TICKS * experts)
    return jnp.pad(table, ((0, 0), (0, LANES - TICKS * experts))).astype(BF16)


def per_device(
    tokens, norm_gain, gate_weight, up_weight, down_weight, block_scales, routes, route_weights
):
    experts = lax.axis_size("expert") // SPLIT
    state = tokens[0]
    table = weights_table(routes[0], route_weights[0], experts)
    rows = jnp.concatenate([state, table], axis=1)

    factors = jnp.exp2(block_scales[0].astype(F32)).reshape(-1)
    rows, factors = lax.optimization_barrier((rows, factors))
    own = scaled_weights(gate_weight[0], up_weight[0], down_weight[0], factors)
    weights = (own, other_core(own))

    held_table = None
    for tick in range(TICKS):
        pieces = gather_second(gather_first(rows))
        outs, held_table = experts_share(
            pieces, norm_gain, weights, held_table, tick * experts
        )
        rows = state = sum_to_next(state, outs)
    return state[None]


def solution(mesh):
    in_specs = (
        P("section", "expert", None),
        P("section", None),
        P("section", None, "expert"),
        P("section", None, "expert"),
        P("section", "expert", None),
        P("section", None, None, "expert"),
        P("section", None, "expert", None),
        P("section", None, "expert", None),
    )
    out_specs = P("section", "expert", None)
    return jax.shard_map(
        per_device, mesh=mesh, in_specs=in_specs, out_specs=out_specs, check_vma=False
    )
```

```python
import jax
import jax.numpy as jnp
from jax import lax
from jax.experimental import pallas as pl
from jax.experimental.pallas import tpu as pltpu
from jax.sharding import PartitionSpec as P

SPLIT = 4
TICKS = 2
LANES = 128
VMEM_LIMIT = 16 * 1024 * 1024
AHEAD = 4
F32 = jnp.float32
BF16 = jnp.bfloat16


def along_z(shard, by):
    length = lax.axis_size("expert")
    return lax.ppermute(
        shard, "expert", [(i, (i + 2 * by) % length) for i in range(length)]
    )


def other_core(shard):
    length = lax.axis_size("expert")
    return lax.ppermute(shard, "expert", [(i, i ^ 1) for i in range(length)])


def to_next_section(shard, by):
    sections, length = lax.axis_size("section"), lax.axis_size("expert")
    pairs = [
        (s * length + e, (s + 1) % sections * length + (e + 2 * by) % length)
        for s in range(sections)
        for e in range(length)
    ]
    return lax.ppermute(shard, ("section", "expert"), pairs)


def cut_of(width):
    return width // LANES // 2 * LANES


def gather_first(block):
    far_back, far_ahead = along_z(block, 2), along_z(block, -2)
    return [block, along_z(block, 1), along_z(block, -1), far_back, far_ahead]


def gather_second(first):
    far_back, far_ahead = first[3], first[4]
    cut = cut_of(far_back.shape[1])
    return first + [
        along_z(far_back, 1),
        along_z(far_ahead, -1),
        along_z(far_back[:, :cut], 2),
        along_z(far_ahead[:, cut:], -2),
    ]


def sum_to_next(state, outs):
    far = [
        along_z(outs[7], -2),
        along_z(outs[8], 2),
        along_z(outs[5], -1),
        along_z(outs[6], 1),
    ]
    far[0], last = lax.optimization_barrier((far[0], outs[2]))
    near = [along_z(outs[1], -1), along_z(last, 1)]
    back, ahead = join_far(outs[3], outs[4], *far)
    parts = [to_next_section(back, -2), to_next_section(ahead, 2)]
    parts.append(to_next_section(join_near(state, outs[0], *near), 0))
    return sum(part.astype(F32) for part in parts).astype(BF16)


def join_call(kernel, name, n_out, *operands):
    rows, width = operands[0].shape
    return pl.pallas_call(
        kernel,
        out_shape=[jax.ShapeDtypeStruct((rows, width), BF16)] * n_out,
        compiler_params=pltpu.CompilerParams(vmem_limit_bytes=VMEM_LIMIT),
        cost_estimate=pl.CostEstimate(
            flops=4 * rows * width, bytes_accessed=12 * rows * width, transcendentals=0
        ),
        name=name,
    )(*operands)


def join_far(back, ahead, left, right, back_3, ahead_3):
    width = back.shape[1]
    cut = cut_of(width)

    def kernel(back, ahead, left, right, b3, a3, back_out, ahead_out):
        lo, hi = slice(0, cut), slice(cut, width)
        f = lambda ref, cols: ref[:, cols].astype(F32)
        back_out[:, lo] = (f(back, lo) + f(b3, lo) + left[...].astype(F32)).astype(BF16)
        back_out[:, hi] = (f(back, hi) + f(b3, hi)).astype(BF16)
        ahead_out[:, lo] = (f(ahead, lo) + f(a3, lo)).astype(BF16)
        ahead_out[:, hi] = (f(ahead, hi) + f(a3, hi) + right[...].astype(F32)).astype(BF16)

    return join_call(kernel, "join_far", 2, back, ahead, left, right, back_3, ahead_3)


def join_near(state, own, back, ahead):
    def kernel(state, own, back, ahead, out):
        f = lambda ref: ref[...].astype(F32)
        out[...] = (f(state) + (f(own) + f(back) + f(ahead))).astype(BF16)

    return join_call(kernel, "join_near", 1, state, own, back, ahead)[0]


def load_rows(pieces, gain, rows_ref, squares_ref):
    height = pieces[0].shape[0]
    width = gain.shape[1]
    cut = cut_of(pieces[0].shape[1])

    def put(ref, at, lo, hi, base):
        held = None
        for c in range(lo, hi, LANES):
            x = ref[:, c - base : c - base + LANES].astype(F32)
            held = x * x if held is None else held + x * x
            rows_ref[at : at + height, c : c + LANES] = (
                x * gain[:, c : c + LANES]
            ).astype(BF16)
        return held

    for n in range(8):
        at = n * height
        if n < 7:
            held = put(pieces[n], at, 0, width, 0)
        else:
            held = put(pieces[7], at, 0, cut, 0) + put(pieces[8], at, cut, width, cut)
        squares_ref[at : at + height, :] = held


def load_table(pieces, width, table_ref):
    height = pieces[0].shape[0]
    cut = cut_of(pieces[0].shape[1])
    for n in range(8):
        ref, lo = (pieces[n], width) if n < 7 else (pieces[8], width - cut)
        table_ref[n * height : (n + 1) * height, :] = ref[:, lo : lo + LANES].astype(F32)


def scaled(block, factor):
    return block * jnp.full(block.shape, factor, F32).astype(BF16)


def scaled_weights(arrays, factors, first):
    side, width = min(arrays[0].shape), max(arrays[0].shape)
    per_block, blocks, strips = side // LANES, width // side, width // LANES
    group = max(n for n in (1, 2, 4) if blocks % n == 0)
    groups = [(n, at) for n in range(len(arrays)) for at in range(0, blocks, group)]

    def kernel(f_ref, *refs):
        ins, out_ref, sems = refs[: len(arrays)], refs[-2], refs[-1]

        def copies(n, at):
            if ins[n].shape[0] == width:
                src = ins[n].at[pl.ds(at * side, group * side), :]
                dst = out_ref.at[pl.ds(n * width + at * side, group * side), :]
                return [pltpu.make_async_copy(src, dst, sems.at[n, at])]
            return [
                pltpu.make_async_copy(
                    ins[n].at[:, pl.ds(j * side, side)],
                    out_ref.at[pl.ds(n * width + j * side, side), :],
                    sems.at[n, j],
                )
                for j in range(at, at + group)
            ]

        def scale(n, at):
            tall = ins[n].shape[0] == width
            for j in range(at, at + group):
                for a in range(per_block):
                    for b in range(per_block):
                        along, across = (a, b) if tall else (b, a)
                        strip = (first + n) * strips + j * per_block + along
                        row = n * width + j * side + a * LANES
                        place = (slice(row, row + LANES), slice(b * LANES, (b + 1) * LANES))
                        out_ref[place] = scaled(out_ref[place], f_ref[strip * per_block + across])

        for n in range(len(groups) + AHEAD):
            if n < len(groups):
                for copy in copies(*groups[n]):
                    copy.start()
            if n >= AHEAD:
                for copy in copies(*groups[n - AHEAD]):
                    copy.wait()
                scale(*groups[n - AHEAD])

    return pl.pallas_call(
        kernel,
        in_specs=[pl.BlockSpec(memory_space=pltpu.SMEM)]
        + [pl.BlockSpec(memory_space=pltpu.HBM)] * len(arrays),
        out_specs=pl.BlockSpec(memory_space=pltpu.VMEM),
        out_shape=jax.ShapeDtypeStruct((len(arrays) * width, side), BF16),
        scratch_shapes=[pltpu.SemaphoreType.DMA((len(arrays), blocks))],
        compiler_params=pltpu.CompilerParams(vmem_limit_bytes=VMEM_LIMIT),
        cost_estimate=pl.CostEstimate(
            flops=len(arrays) * width * side,
            bytes_accessed=4 * len(arrays) * width * side,
            transcendentals=0,
        ),
        name="scaled_weights",
    )(factors, *(pltpu.with_memory_space_constraint(w, pltpu.HBM) for w in arrays))


def experts_share(pieces, gain, weights, table, first_lane):
    width = gain.shape[1]
    side = weights[0].shape[1]
    height = pieces[0].shape[0]
    rows = 8 * height
    cut = cut_of(width)
    tile = side * max(n for n in (1, 2, 4) if width // side % n == 0)
    n_pieces = len(pieces)
    new_table = table is None

    def kernel(*refs):
        ins, gain_ref = refs[:n_pieces], refs[n_pieces]
        cores, rest = refs[n_pieces + 1 : n_pieces + 3], refs[n_pieces + 3 :]
        if not new_table:
            table_in, rest = rest[0], rest[1:]
        outs, table_ref = rest[:9], rest[9]
        rows_ref, squares_ref, hidden_ref = rest[10:]

        load_rows(ins, gain_ref, rows_ref, squares_ref)
        if new_table:
            load_table(ins, width, table_ref)
        else:
            table_ref[...] = table_in[...]
        mean = jnp.sum(squares_ref[...], axis=-1, keepdims=True) / width
        factor = lax.rsqrt(mean + 1e-06)
        lane = lax.broadcasted_iota(jnp.int32, (rows, LANES), 1)
        own_lane = first_lane + lax.div(lax.axis_index("expert"), SPLIT)
        picked = jnp.where(lane == own_lane, table_ref[...], 0.0)
        weight = jnp.sum(picked, axis=-1, keepdims=True)

        for core, ref in enumerate(cores):
            gate = jnp.dot(rows_ref[...], ref[:width, :], preferred_element_type=F32)
            up = jnp.dot(rows_ref[...], ref[width : 2 * width, :], preferred_element_type=F32)
            gate, up = gate * factor, up * factor
            hidden_ref[:, core * side : (core + 1) * side] = (
                gate / (1.0 + jnp.exp(-gate)) * up
            ).astype(BF16)

        for lo in range(0, width, side):
            product = sum(
                jnp.dot(
                    hidden_ref[:, core * side : (core + 1) * side],
                    ref[2 * width + lo : 2 * width + lo + side, :],
                    preferred_element_type=F32,
                )
                for core, ref in enumerate(cores)
            )
            product = (product * weight).astype(BF16)
            hi = lo + side
            for n in range(7):
                outs[n][:, lo:hi] = product[n * height : (n + 1) * height, :]
            last = product[7 * height :, :]
            if lo < cut:
                outs[7][:, lo : min(hi, cut)] = last[:, : min(hi, cut) - lo]
            if hi > cut:
                outs[8][:, max(lo, cut) - cut : hi - cut] = last[:, max(lo, cut) - lo :]

    vmem = pl.BlockSpec(memory_space=pltpu.VMEM)
    tables = [] if new_table else [table]
    held = [pltpu.with_memory_space_constraint(w, pltpu.VMEM) for w in weights]
    operands = [*pieces, gain, *held, *tables]
    out_sizes = [(height, width)] * 7 + [(height, cut), (height, width - cut)]
    results = pl.pallas_call(
        kernel,
        in_specs=[vmem] * len(operands),
        out_specs=[vmem] * 10,
        out_shape=[jax.ShapeDtypeStruct(s, BF16) for s in out_sizes]
        + [jax.ShapeDtypeStruct((rows, LANES), F32)],
        scratch_shapes=[
            pltpu.VMEM((rows, width), BF16),
            pltpu.VMEM((rows, LANES), F32),
            pltpu.VMEM((rows, 2 * side), BF16),
        ],
        compiler_params=pltpu.CompilerParams(vmem_limit_bytes=VMEM_LIMIT),
        cost_estimate=pl.CostEstimate(
            flops=12 * rows * width * side,
            bytes_accessed=12 * width * side,
            transcendentals=2 * rows * side,
        ),
        name="experts_share",
    )(*operands)
    return results[:9], results[9]


def weights_table(routes, route_weights, experts):
    ids = jnp.arange(experts, dtype=jnp.int32)
    matches = (routes[..., None] == ids).astype(F32)
    table = jnp.sum(matches * route_weights.astype(F32)[..., None], axis=2)
    table = table.transpose(1, 0, 2).reshape(table.shape[1], TICKS * experts)
    return jnp.pad(table, ((0, 0), (0, LANES - TICKS * experts))).astype(BF16)


def per_device(
    tokens, norm_gain, gate_weight, up_weight, down_weight, block_scales, routes, route_weights
):
    experts = lax.axis_size("expert") // SPLIT
    state = tokens[0]
    table = weights_table(routes[0], route_weights[0], experts)
    rows = jnp.concatenate([state, table], axis=1)

    factors = jnp.exp2(block_scales[0].astype(F32)).reshape(-1)
    rows, factors = lax.optimization_barrier((rows, factors))
    own = scaled_weights((gate_weight[0], up_weight[0], down_weight[0]), factors, 0)
    weights = (own, other_core(own))

    held_table = None
    for tick in range(TICKS):
        pieces = gather_second(gather_first(rows))
        outs, held_table = experts_share(
            pieces, norm_gain, weights, held_table, tick * experts
        )
        rows = state = sum_to_next(state, outs)
    return state[None]


def solution(mesh):
    in_specs = (
        P("section", "expert", None),
        P("section", None),
        P("section", None, "expert"),
        P("section", None, "expert"),
        P("section", "expert", None),
        P("section", None, None, "expert"),
        P("section", None, "expert", None),
        P("section", None, "expert", None),
    )
    out_specs = P("section", "expert", None)
    return jax.shard_map(
        per_device, mesh=mesh, in_specs=in_specs, out_specs=out_specs, check_vma=False
    )
```

```python
import jax
import jax.numpy as jnp
from jax import lax
from jax.experimental import pallas as pl
from jax.experimental.pallas import tpu as pltpu
from jax.sharding import PartitionSpec as P

SPLIT = 4
TICKS = 2
LANES = 128
VMEM_LIMIT = 16 * 1024 * 1024
AHEAD = 10
F32 = jnp.float32
BF16 = jnp.bfloat16


def along_z(shard, by):
    length = lax.axis_size("expert")
    return lax.ppermute(
        shard, "expert", [(i, (i + 2 * by) % length) for i in range(length)]
    )


def other_core(shard):
    length = lax.axis_size("expert")
    return lax.ppermute(shard, "expert", [(i, i ^ 1) for i in range(length)])


def to_next_section(shard, by):
    sections, length = lax.axis_size("section"), lax.axis_size("expert")
    pairs = [
        (s * length + e, (s + 1) % sections * length + (e + 2 * by) % length)
        for s in range(sections)
        for e in range(length)
    ]
    return lax.ppermute(shard, ("section", "expert"), pairs)


def cut_of(width):
    return width // LANES // 2 * LANES


def gather_first(block):
    far_back, far_ahead = along_z(block, 2), along_z(block, -2)
    return [block, along_z(block, 1), along_z(block, -1), far_back, far_ahead]


def gather_second(first):
    far_back, far_ahead = first[3], first[4]
    cut = cut_of(far_back.shape[1])
    return first + [
        along_z(far_back, 1),
        along_z(far_ahead, -1),
        along_z(far_back[:, :cut], 2),
        along_z(far_ahead[:, cut:], -2),
    ]


def sum_to_next(state, outs):
    far = [
        along_z(outs[7], -2),
        along_z(outs[8], 2),
        along_z(outs[5], -1),
        along_z(outs[6], 1),
    ]
    far[0], near_back = lax.optimization_barrier((far[0], outs[1]))
    far[1], near_ahead = lax.optimization_barrier((far[1], outs[2]))
    near = [along_z(near_back, -1), along_z(near_ahead, 1)]
    back, ahead = join_far(outs[3], outs[4], *far)
    parts = [to_next_section(back, -2), to_next_section(ahead, 2)]
    parts.append(to_next_section(join_near(state, outs[0], *near), 0))
    return sum(part.astype(F32) for part in parts).astype(BF16)


def join_call(kernel, name, n_out, *operands):
    rows, width = operands[0].shape
    return pl.pallas_call(
        kernel,
        out_shape=[jax.ShapeDtypeStruct((rows, width), BF16)] * n_out,
        compiler_params=pltpu.CompilerParams(vmem_limit_bytes=VMEM_LIMIT),
        cost_estimate=pl.CostEstimate(
            flops=4 * rows * width, bytes_accessed=12 * rows * width, transcendentals=0
        ),
        name=name,
    )(*operands)


def join_far(back, ahead, left, right, back_3, ahead_3):
    width = back.shape[1]
    cut = cut_of(width)

    def kernel(back, ahead, left, right, b3, a3, back_out, ahead_out):
        lo, hi = slice(0, cut), slice(cut, width)
        f = lambda ref, cols: ref[:, cols].astype(F32)
        back_out[:, lo] = (f(back, lo) + f(b3, lo) + left[...].astype(F32)).astype(BF16)
        back_out[:, hi] = (f(back, hi) + f(b3, hi)).astype(BF16)
        ahead_out[:, lo] = (f(ahead, lo) + f(a3, lo)).astype(BF16)
        ahead_out[:, hi] = (f(ahead, hi) + f(a3, hi) + right[...].astype(F32)).astype(BF16)

    return join_call(kernel, "join_far", 2, back, ahead, left, right, back_3, ahead_3)


def join_near(state, own, back, ahead):
    def kernel(state, own, back, ahead, out):
        f = lambda ref: ref[...].astype(F32)
        out[...] = (f(state) + (f(own) + f(back) + f(ahead))).astype(BF16)

    return join_call(kernel, "join_near", 1, state, own, back, ahead)[0]


def load_rows(pieces, gain, rows_ref, squares_ref):
    height = pieces[0].shape[0]
    width = gain.shape[1]
    cut = cut_of(pieces[0].shape[1])

    def put(ref, at, lo, hi, base):
        held = None
        for c in range(lo, hi, LANES):
            x = ref[:, c - base : c - base + LANES].astype(F32)
            held = x * x if held is None else held + x * x
            rows_ref[at : at + height, c : c + LANES] = (
                x * gain[:, c : c + LANES]
            ).astype(BF16)
        return held

    for n in range(8):
        at = n * height
        if n < 7:
            held = put(pieces[n], at, 0, width, 0)
        else:
            held = put(pieces[7], at, 0, cut, 0) + put(pieces[8], at, cut, width, cut)
        squares_ref[at : at + height, :] = held


def load_table(pieces, width, table_ref):
    height = pieces[0].shape[0]
    cut = cut_of(pieces[0].shape[1])
    for n in range(8):
        ref, lo = (pieces[n], width) if n < 7 else (pieces[8], width - cut)
        table_ref[n * height : (n + 1) * height, :] = ref[:, lo : lo + LANES].astype(F32)


def scaled(block, factor):
    return block * jnp.full(block.shape, factor, F32).astype(BF16)


def prepare(tokens, routes, route_weights, exponents, arrays, experts):
    height = tokens.shape[0]
    side, width = min(arrays[0].shape), max(arrays[0].shape)
    per_block, blocks, strips = side // LANES, width // side, width // LANES
    group = max(n for n in (1, 2, 4) if blocks % n == 0)
    groups = [(n, at) for n in range(len(arrays)) for at in range(0, blocks, group)]

    def kernel(exp_ref, tokens_ref, routes_ref, route_weights_ref, *refs):
        ins, rows_out, out_ref, sems = refs[: len(arrays)], *refs[len(arrays) :]

        def copies(n, at):
            if ins[n].shape[0] == width:
                src = ins[n].at[pl.ds(at * side, group * side), :]
                dst = out_ref.at[pl.ds(n * width + at * side, group * side), :]
                return [pltpu.make_async_copy(src, dst, sems.at[n, at])]
            return [
                pltpu.make_async_copy(
                    ins[n].at[:, pl.ds(j * side, side)],
                    out_ref.at[pl.ds(n * width + j * side, side), :],
                    sems.at[n, j],
                )
                for j in range(at, at + group)
            ]

        def scale(n, at):
            tall = ins[n].shape[0] == width
            for j in range(at, at + group):
                for a in range(per_block):
                    for b in range(per_block):
                        along, across = (a, b) if tall else (b, a)
                        strip = n * strips + j * per_block + along
                        exponent = exp_ref[strip * per_block + across]
                        factor = jnp.left_shift(1, exponent + 16).astype(F32) * 2.0**-16
                        row = n * width + j * side + a * LANES
                        place = (slice(row, row + LANES), slice(b * LANES, (b + 1) * LANES))
                        out_ref[place] = scaled(out_ref[place], factor)

        for n in range(len(groups) + AHEAD):
            if n < len(groups):
                for copy in copies(*groups[n]):
                    copy.start()
            if n == AHEAD:
                lane = lax.broadcasted_iota(jnp.int32, (height, LANES), 1)
                table = jnp.zeros((height, LANES), F32)
                for step in range(TICKS):
                    for k in range(routes.shape[-1]):
                        named = routes_ref[step, :, k : k + 1] + step * experts
                        weight = route_weights_ref[step, :, k : k + 1].astype(F32)
                        table += jnp.where(lane == named, weight, 0.0)
                rows_out[:, :width] = tokens_ref[...]
                rows_out[:, width:] = table.astype(BF16)
            if n >= AHEAD:
                for copy in copies(*groups[n - AHEAD]):
                    copy.wait()
                scale(*groups[n - AHEAD])

    vmem = pl.BlockSpec(memory_space=pltpu.VMEM)
    return pl.pallas_call(
        kernel,
        in_specs=[pl.BlockSpec(memory_space=pltpu.SMEM)]
        + [vmem] * 3
        + [pl.BlockSpec(memory_space=pltpu.HBM)] * len(arrays),
        out_specs=[vmem] * 2,
        out_shape=[
            jax.ShapeDtypeStruct((height, width + LANES), BF16),
            jax.ShapeDtypeStruct((len(arrays) * width, side), BF16),
        ],
        scratch_shapes=[pltpu.SemaphoreType.DMA((len(arrays), blocks))],
        compiler_params=pltpu.CompilerParams(vmem_limit_bytes=VMEM_LIMIT),
        cost_estimate=pl.CostEstimate(
            flops=len(arrays) * width * side,
            bytes_accessed=4 * len(arrays) * width * side,
            transcendentals=0,
        ),
        name="prepare",
    )(
        exponents,
        tokens,
        routes,
        route_weights,
        *(pltpu.with_memory_space_constraint(w, pltpu.HBM) for w in arrays),
    )


def experts_share(pieces, gain, weights, table, first_lane):
    width = gain.shape[1]
    side = weights[0].shape[1]
    height = pieces[0].shape[0]
    rows = 8 * height
    cut = cut_of(width)
    tile = side * max(n for n in (1, 2, 4) if width // side % n == 0)
    n_pieces = len(pieces)
    new_table = table is None

    def kernel(*refs):
        ins, gain_ref = refs[:n_pieces], refs[n_pieces]
        cores, rest = refs[n_pieces + 1 : n_pieces + 3], refs[n_pieces + 3 :]
        if not new_table:
            table_in, rest = rest[0], rest[1:]
        outs, table_ref = rest[:9], rest[9]
        rows_ref, squares_ref, hidden_ref = rest[10:]

        load_rows(ins, gain_ref, rows_ref, squares_ref)
        if new_table:
            load_table(ins, width, table_ref)
        else:
            table_ref[...] = table_in[...]
        mean = jnp.sum(squares_ref[...], axis=-1, keepdims=True) / width
        factor = lax.rsqrt(mean + 1e-06)
        lane = lax.broadcasted_iota(jnp.int32, (rows, LANES), 1)
        own_lane = first_lane + lax.div(lax.axis_index("expert"), SPLIT)
        picked = jnp.where(lane == own_lane, table_ref[...], 0.0)
        weight = jnp.sum(picked, axis=-1, keepdims=True)

        for core, ref in enumerate(cores):
            gate = jnp.dot(rows_ref[...], ref[:width, :], preferred_element_type=F32)
            up = jnp.dot(rows_ref[...], ref[width : 2 * width, :], preferred_element_type=F32)
            gate, up = gate * factor, up * factor
            hidden_ref[:, core * side : (core + 1) * side] = (
                gate / (1.0 + jnp.exp(-gate)) * up
            ).astype(BF16)

        for lo in range(0, width, side):
            product = sum(
                jnp.dot(
                    hidden_ref[:, core * side : (core + 1) * side],
                    ref[2 * width + lo : 2 * width + lo + side, :],
                    preferred_element_type=F32,
                )
                for core, ref in enumerate(cores)
            )
            product = (product * weight).astype(BF16)
            hi = lo + side
            for n in range(7):
                outs[n][:, lo:hi] = product[n * height : (n + 1) * height, :]
            last = product[7 * height :, :]
            if lo < cut:
                outs[7][:, lo : min(hi, cut)] = last[:, : min(hi, cut) - lo]
            if hi > cut:
                outs[8][:, max(lo, cut) - cut : hi - cut] = last[:, max(lo, cut) - lo :]

    vmem = pl.BlockSpec(memory_space=pltpu.VMEM)
    tables = [] if new_table else [table]
    held = [pltpu.with_memory_space_constraint(w, pltpu.VMEM) for w in weights]
    operands = [*pieces, gain, *held, *tables]
    out_sizes = [(height, width)] * 7 + [(height, cut), (height, width - cut)]
    results = pl.pallas_call(
        kernel,
        in_specs=[vmem] * len(operands),
        out_specs=[vmem] * 10,
        out_shape=[jax.ShapeDtypeStruct(s, BF16) for s in out_sizes]
        + [jax.ShapeDtypeStruct((rows, LANES), F32)],
        scratch_shapes=[
            pltpu.VMEM((rows, width), BF16),
            pltpu.VMEM((rows, LANES), F32),
            pltpu.VMEM((rows, 2 * side), BF16),
        ],
        compiler_params=pltpu.CompilerParams(vmem_limit_bytes=VMEM_LIMIT),
        cost_estimate=pl.CostEstimate(
            flops=12 * rows * width * side,
            bytes_accessed=12 * width * side,
            transcendentals=2 * rows * side,
        ),
        name="experts_share",
    )(*operands)
    return results[:9], results[9]


def per_device(
    tokens, norm_gain, gate_weight, up_weight, down_weight, block_scales, routes, route_weights
):
    experts = lax.axis_size("expert") // SPLIT
    state = tokens[0]
    rows, own = prepare(
        state,
        routes[0],
        route_weights[0],
        block_scales[0].reshape(-1),
        (gate_weight[0], up_weight[0], down_weight[0]),
        experts,
    )
    weights = (own, other_core(own))

    held_table = None
    for tick in range(TICKS):
        pieces = gather_second(gather_first(rows))
        outs, held_table = experts_share(
            pieces, norm_gain, weights, held_table, tick * experts
        )
        rows = state = sum_to_next(state, outs)
    return state[None]


def solution(mesh):
    in_specs = (
        P("section", "expert", None),
        P("section", None),
        P("section", None, "expert"),
        P("section", None, "expert"),
        P("section", "expert", None),
        P("section", None, None, "expert"),
        P("section", None, "expert", None),
        P("section", None, "expert", None),
    )
    out_specs = P("section", "expert", None)
    return jax.shard_map(
        per_device, mesh=mesh, in_specs=in_specs, out_specs=out_specs, check_vma=False
    )
```

```python
import jax
import jax.numpy as jnp
from jax import lax
from jax.experimental import pallas as pl
from jax.experimental.pallas import tpu as pltpu
from jax.sharding import PartitionSpec as P

SPLIT = 4
TICKS = 2
LANES = 128
VMEM_LIMIT = 16 * 1024 * 1024
AHEAD = 10
F32 = jnp.float32
BF16 = jnp.bfloat16


def along_z(shard, by):
    length = lax.axis_size("expert")
    return lax.ppermute(
        shard, "expert", [(i, (i + 2 * by) % length) for i in range(length)]
    )


def other_core(shard):
    length = lax.axis_size("expert")
    return lax.ppermute(shard, "expert", [(i, i ^ 1) for i in range(length)])


def to_next_section(shard, by):
    sections, length = lax.axis_size("section"), lax.axis_size("expert")
    pairs = [
        (s * length + e, (s + 1) % sections * length + (e + 2 * by) % length)
        for s in range(sections)
        for e in range(length)
    ]
    return lax.ppermute(shard, ("section", "expert"), pairs)


def cut_of(width):
    return width // LANES // 2 * LANES


def gather_first(block):
    far_back, far_ahead = along_z(block, 2), along_z(block, -2)
    return [block, along_z(block, 1), along_z(block, -1), far_back, far_ahead]


def gather_second(first):
    far_back, far_ahead = first[3], first[4]
    cut = cut_of(far_back.shape[1])
    return first + [
        along_z(far_back, 1),
        along_z(far_ahead, -1),
        along_z(far_back[:, :cut], 2),
        along_z(far_ahead[:, cut:], -2),
    ]


def sum_to_next(outs):
    far = [
        along_z(outs[7], -2),
        along_z(outs[8], 2),
        along_z(outs[5], -1),
        along_z(outs[6], 1),
    ]
    far[0], near_back = lax.optimization_barrier((far[0], outs[1]))
    far[1], near_ahead = lax.optimization_barrier((far[1], outs[2]))
    parts = [
        to_next_section(outs[0], 0),
        to_next_section(near_back, -1),
        to_next_section(near_ahead, 1),
    ]
    back, ahead = join_far(outs[3], outs[4], *far)
    parts += [to_next_section(back, -2), to_next_section(ahead, 2)]
    return sum(part.astype(F32) for part in parts).astype(BF16)


def join_far(back, ahead, left, right, back_3, ahead_3):
    width = back.shape[1]
    cut = cut_of(width)

    def kernel(back, ahead, left, right, b3, a3, back_out, ahead_out):
        lo, hi = slice(0, cut), slice(cut, width)
        f = lambda ref, cols: ref[:, cols].astype(F32)
        back_out[:, lo] = (f(back, lo) + f(b3, lo) + left[...].astype(F32)).astype(BF16)
        back_out[:, hi] = (f(back, hi) + f(b3, hi)).astype(BF16)
        ahead_out[:, lo] = (f(ahead, lo) + f(a3, lo)).astype(BF16)
        ahead_out[:, hi] = (f(ahead, hi) + f(a3, hi) + right[...].astype(F32)).astype(BF16)

    rows = back.shape[0]
    return pl.pallas_call(
        kernel,
        out_shape=[jax.ShapeDtypeStruct((rows, width), BF16)] * 2,
        compiler_params=pltpu.CompilerParams(vmem_limit_bytes=VMEM_LIMIT),
        cost_estimate=pl.CostEstimate(
            flops=6 * rows * width, bytes_accessed=14 * rows * width, transcendentals=0
        ),
        name="join_far",
    )(back, ahead, left, right, back_3, ahead_3)


def load_rows(pieces, gain, rows_ref, squares_ref):
    height = pieces[0].shape[0]
    width = gain.shape[1]
    cut = cut_of(pieces[0].shape[1])

    def put(ref, at, lo, hi, base):
        held = None
        for c in range(lo, hi, LANES):
            x = ref[:, c - base : c - base + LANES].astype(F32)
            held = x * x if held is None else held + x * x
            rows_ref[at : at + height, c : c + LANES] = (
                x * gain[:, c : c + LANES]
            ).astype(BF16)
        return held

    for n in range(8):
        at = n * height
        if n < 7:
            held = put(pieces[n], at, 0, width, 0)
        else:
            held = put(pieces[7], at, 0, cut, 0) + put(pieces[8], at, cut, width, cut)
        squares_ref[at : at + height, :] = held


def load_table(pieces, width, table_ref):
    height = pieces[0].shape[0]
    cut = cut_of(pieces[0].shape[1])
    for n in range(8):
        ref, lo = (pieces[n], width) if n < 7 else (pieces[8], width - cut)
        table_ref[n * height : (n + 1) * height, :] = ref[:, lo : lo + LANES].astype(F32)


def scaled(block, factor):
    return block * jnp.full(block.shape, factor, F32).astype(BF16)


def prepare(tokens, routes, route_weights, exponents, arrays, experts):
    height = tokens.shape[0]
    side, width = min(arrays[0].shape), max(arrays[0].shape)
    per_block, blocks = side // LANES, width // side
    group = max(n for n in (1, 2, 4) if blocks % n == 0)
    groups = [(n, at) for n in range(len(arrays)) for at in range(0, blocks, group)]

    def kernel(exp_ref, tokens_ref, routes_ref, route_weights_ref, *refs):
        ins, rows_out, out_ref, sems, rows_sem = refs[: len(arrays)], *refs[len(arrays) :]

        def copies(n, at):
            if ins[n].shape[0] == width:
                src = ins[n].at[pl.ds(at * side, group * side), :]
                dst = out_ref.at[pl.ds(n * width + at * side, group * side), :]
                return [pltpu.make_async_copy(src, dst, sems.at[n, at])]
            return [
                pltpu.make_async_copy(
                    ins[n].at[:, pl.ds(j * side, side)],
                    out_ref.at[pl.ds(n * width + j * side, side), :],
                    sems.at[n, j],
                )
                for j in range(at, at + group)
            ]

        def scale(n, at):
            tall = ins[n].shape[0] == width
            for j in range(at, at + group):
                for a in range(per_block):
                    for b in range(per_block):
                        along, across = (a, b) if tall else (b, a)
                        strip = j * per_block + along
                        exponent = exp_ref[n, across, strip]
                        factor = jnp.left_shift(1, exponent + 16).astype(F32) * 2.0**-16
                        row = n * width + j * side + a * LANES
                        place = (slice(row, row + LANES), slice(b * LANES, (b + 1) * LANES))
                        out_ref[place] = scaled(out_ref[place], factor)

        rows_copy = pltpu.make_async_copy(tokens_ref, rows_out.at[:, pl.ds(0, width)], rows_sem)
        rows_copy.start()
        for n in range(len(groups) + AHEAD):
            if n < len(groups):
                for copy in copies(*groups[n]):
                    copy.start()
            if n == AHEAD:
                lane = lax.broadcasted_iota(jnp.int32, (LANES, height), 0)
                table = jnp.zeros((LANES, height), F32)
                for step in range(TICKS):
                    for k in range(routes.shape[1]):
                        named = routes_ref[step, k : k + 1, :] + step * experts
                        weight = route_weights_ref[step].astype(F32)[k : k + 1, :]
                        table += jnp.where(lane == named, weight, 0.0)
                rows_out[:, width:] = table.T.astype(BF16)
            if n >= AHEAD:
                for copy in copies(*groups[n - AHEAD]):
                    copy.wait()
                scale(*groups[n - AHEAD])
        rows_copy.wait()

    vmem, hbm = (pl.BlockSpec(memory_space=space) for space in (pltpu.VMEM, pltpu.HBM))
    return pl.pallas_call(
        kernel,
        in_specs=[pl.BlockSpec(memory_space=pltpu.SMEM), hbm, vmem, vmem] + [hbm] * len(arrays),
        out_specs=[vmem] * 2,
        out_shape=[
            jax.ShapeDtypeStruct((height, width + LANES), BF16),
            jax.ShapeDtypeStruct((len(arrays) * width, side), BF16),
        ],
        scratch_shapes=[pltpu.SemaphoreType.DMA((len(arrays), blocks)), pltpu.SemaphoreType.DMA],
        compiler_params=pltpu.CompilerParams(vmem_limit_bytes=VMEM_LIMIT),
        cost_estimate=pl.CostEstimate(
            flops=len(arrays) * width * side,
            bytes_accessed=4 * len(arrays) * width * side,
            transcendentals=0,
        ),
        name="prepare",
    )(
        exponents,
        pltpu.with_memory_space_constraint(tokens, pltpu.HBM),
        routes,
        route_weights,
        *(pltpu.with_memory_space_constraint(w, pltpu.HBM) for w in arrays),
    )


def experts_share(pieces, gain, weights, table, first_lane):
    width = gain.shape[1]
    side = weights[0].shape[1]
    height = pieces[0].shape[0]
    rows = 8 * height
    cut = cut_of(width)
    tile = side * max(n for n in (1, 2, 4) if width // side % n == 0)
    n_pieces = len(pieces)
    new_table = table is None

    def kernel(*refs):
        ins, gain_ref = refs[:n_pieces], refs[n_pieces]
        cores, rest = refs[n_pieces + 1 : n_pieces + 3], refs[n_pieces + 3 :]
        if not new_table:
            table_in, rest = rest[0], rest[1:]
        outs, table_ref = rest[:9], rest[9]
        rows_ref, squares_ref, hidden_ref = rest[10:]

        load_rows(ins, gain_ref, rows_ref, squares_ref)
        if new_table:
            load_table(ins, width, table_ref)
        else:
            table_ref[...] = table_in[...]
        mean = jnp.sum(squares_ref[...], axis=-1, keepdims=True) / width
        factor = lax.rsqrt(mean + 1e-06)
        lane = lax.broadcasted_iota(jnp.int32, (rows, LANES), 1)
        own_lane = first_lane + lax.div(lax.axis_index("expert"), SPLIT)
        picked = jnp.where(lane == own_lane, table_ref[...], 0.0)
        weight = jnp.sum(picked, axis=-1, keepdims=True)

        for core, ref in enumerate(cores):
            gate = jnp.dot(rows_ref[...], ref[:width, :], preferred_element_type=F32)
            up = jnp.dot(rows_ref[...], ref[width : 2 * width, :], preferred_element_type=F32)
            gate, up = gate * factor, up * factor
            hidden_ref[:, core * side : (core + 1) * side] = (
                gate / (1.0 + jnp.exp(-gate)) * up
            ).astype(BF16)

        for lo in range(0, width, side):
            product = sum(
                jnp.dot(
                    hidden_ref[:, core * side : (core + 1) * side],
                    ref[2 * width + lo : 2 * width + lo + side, :],
                    preferred_element_type=F32,
                )
                for core, ref in enumerate(cores)
            )
            product = product * weight
            hi = lo + side
            kept = ins[0][:, lo:hi].astype(F32) + product[:height, :]
            outs[0][:, lo:hi] = kept.astype(BF16)
            product = product.astype(BF16)
            for n in range(1, 7):
                outs[n][:, lo:hi] = product[n * height : (n + 1) * height, :]
            last = product[7 * height :, :]
            if lo < cut:
                outs[7][:, lo : min(hi, cut)] = last[:, : min(hi, cut) - lo]
            if hi > cut:
                outs[8][:, max(lo, cut) - cut : hi - cut] = last[:, max(lo, cut) - lo :]

    vmem = pl.BlockSpec(memory_space=pltpu.VMEM)
    tables = [] if new_table else [table]
    held = [pltpu.with_memory_space_constraint(w, pltpu.VMEM) for w in weights]
    operands = [*pieces, gain, *held, *tables]
    out_sizes = [(height, width)] * 7 + [(height, cut), (height, width - cut)]
    results = pl.pallas_call(
        kernel,
        in_specs=[vmem] * len(operands),
        out_specs=[vmem] * 10,
        out_shape=[jax.ShapeDtypeStruct(s, BF16) for s in out_sizes]
        + [jax.ShapeDtypeStruct((rows, LANES), F32)],
        scratch_shapes=[
            pltpu.VMEM((rows, width), BF16),
            pltpu.VMEM((rows, LANES), F32),
            pltpu.VMEM((rows, 2 * side), BF16),
        ],
        compiler_params=pltpu.CompilerParams(vmem_limit_bytes=VMEM_LIMIT),
        cost_estimate=pl.CostEstimate(
            flops=12 * rows * width * side,
            bytes_accessed=12 * width * side,
            transcendentals=2 * rows * side,
        ),
        name="experts_share",
    )(*operands)
    return results[:9], results[9]


def per_device(
    tokens, norm_gain, gate_weight, up_weight, down_weight, block_scales, routes, route_weights
):
    experts = lax.axis_size("expert") // SPLIT
    rows, own = prepare(
        tokens[0],
        routes[0].transpose(0, 2, 1),
        route_weights[0].transpose(0, 2, 1),
        block_scales[0].transpose(0, 2, 1),
        (gate_weight[0], up_weight[0], down_weight[0]),
        experts,
    )
    weights = (own, other_core(own))

    held_table = None
    for tick in range(TICKS):
        pieces = gather_second(gather_first(rows))
        outs, held_table = experts_share(
            pieces, norm_gain, weights, held_table, tick * experts
        )
        rows = sum_to_next(outs)
    return rows[None]


def solution(mesh):
    in_specs = (
        P("section", "expert", None),
        P("section", None),
        P("section", None, "expert"),
        P("section", None, "expert"),
        P("section", "expert", None),
        P("section", None, None, "expert"),
        P("section", None, "expert", None),
        P("section", None, "expert", None),
    )
    out_specs = P("section", "expert", None)
    return jax.shard_map(
        per_device, mesh=mesh, in_specs=in_specs, out_specs=out_specs, check_vma=False
    )
```

```python
import jax
import jax.numpy as jnp
from jax import lax
from jax.experimental import pallas as pl
from jax.experimental.pallas import tpu as pltpu
from jax.sharding import PartitionSpec as P

SPLIT = 4
TICKS = 2
LANES = 128
VMEM_LIMIT = 16 * 1024 * 1024
AHEAD = 10
F32 = jnp.float32
BF16 = jnp.bfloat16


def along_z(shard, by):
    length = lax.axis_size("expert")
    return lax.ppermute(
        shard, "expert", [(i, (i + 2 * by) % length) for i in range(length)]
    )


def other_core(shard):
    length = lax.axis_size("expert")
    return lax.ppermute(shard, "expert", [(i, i ^ 1) for i in range(length)])


def to_next_section(shard, by):
    sections, length = lax.axis_size("section"), lax.axis_size("expert")
    pairs = [
        (s * length + e, (s + 1) % sections * length + (e + 2 * by) % length)
        for s in range(sections)
        for e in range(length)
    ]
    return lax.ppermute(shard, ("section", "expert"), pairs)


def cut_of(width):
    return width // LANES // 2 * LANES


def gather_first(block):
    far_back, far_ahead = along_z(block, 2), along_z(block, -2)
    return [block, along_z(block, 1), along_z(block, -1), far_back, far_ahead]


def gather_second(first):
    far_back, far_ahead = first[3], first[4]
    cut = cut_of(far_back.shape[1])
    return first + [
        along_z(far_back, 1),
        along_z(far_ahead, -1),
        along_z(far_back[:, :cut], 2),
        along_z(far_ahead[:, cut:], -2),
    ]


def sum_to_next(outs):
    far = [
        along_z(outs[7], -2),
        along_z(outs[8], 2),
        along_z(outs[5], -1),
        along_z(outs[6], 1),
    ]
    far[0], near_back = lax.optimization_barrier((far[0], outs[1]))
    far[1], near_ahead = lax.optimization_barrier((far[1], outs[2]))
    near = [along_z(near_back, -1), along_z(near_ahead, 1)]
    back, ahead = join_far(outs[3], outs[4], *far)
    parts = [to_next_section(back, -2), to_next_section(ahead, 2)]
    parts.append(to_next_section(join_near(outs[0], *near), 0))
    return sum(part.astype(F32) for part in parts).astype(BF16)


def join_near(own, back, ahead):
    def kernel(own, back, ahead, out):
        f = lambda ref: ref[...].astype(F32)
        out[...] = (f(own) + (f(back) + f(ahead))).astype(BF16)

    return pl.pallas_call(
        kernel,
        out_shape=jax.ShapeDtypeStruct(own.shape, BF16),
        compiler_params=pltpu.CompilerParams(vmem_limit_bytes=VMEM_LIMIT),
        cost_estimate=pl.CostEstimate(
            flops=2 * own.size, bytes_accessed=8 * own.size, transcendentals=0
        ),
        name="join_near",
    )(own, back, ahead)


def join_far(back, ahead, left, right, back_3, ahead_3):
    width = back.shape[1]
    cut = cut_of(width)

    def kernel(back, ahead, left, right, b3, a3, back_out, ahead_out):
        lo, hi = slice(0, cut), slice(cut, width)
        f = lambda ref, cols: ref[:, cols].astype(F32)
        back_out[:, lo] = (f(back, lo) + f(b3, lo) + left[...].astype(F32)).astype(BF16)
        back_out[:, hi] = (f(back, hi) + f(b3, hi)).astype(BF16)
        ahead_out[:, lo] = (f(ahead, lo) + f(a3, lo)).astype(BF16)
        ahead_out[:, hi] = (f(ahead, hi) + f(a3, hi) + right[...].astype(F32)).astype(BF16)

    rows = back.shape[0]
    return pl.pallas_call(
        kernel,
        out_shape=[jax.ShapeDtypeStruct((rows, width), BF16)] * 2,
        compiler_params=pltpu.CompilerParams(vmem_limit_bytes=VMEM_LIMIT),
        cost_estimate=pl.CostEstimate(
            flops=6 * rows * width, bytes_accessed=14 * rows * width, transcendentals=0
        ),
        name="join_far",
    )(back, ahead, left, right, back_3, ahead_3)


def load_rows(pieces, gain, rows_ref, squares_ref):
    height = pieces[0].shape[0]
    width = gain.shape[1]
    cut = cut_of(pieces[0].shape[1])

    def put(ref, at, lo, hi, base):
        held = None
        for c in range(lo, hi, LANES):
            x = ref[:, c - base : c - base + LANES].astype(F32)
            held = x * x if held is None else held + x * x
            rows_ref[at : at + height, c : c + LANES] = (
                x * gain[:, c : c + LANES]
            ).astype(BF16)
        return held

    for n in range(8):
        at = n * height
        if n < 7:
            held = put(pieces[n], at, 0, width, 0)
        else:
            held = put(pieces[7], at, 0, cut, 0) + put(pieces[8], at, cut, width, cut)
        squares_ref[at : at + height, :] = held


def load_table(pieces, width, table_ref):
    height = pieces[0].shape[0]
    cut = cut_of(pieces[0].shape[1])
    for n in range(8):
        ref, lo = (pieces[n], width) if n < 7 else (pieces[8], width - cut)
        table_ref[n * height : (n + 1) * height, :] = ref[:, lo : lo + LANES].astype(F32)


def scaled(block, factor):
    return block * jnp.full(block.shape, factor, F32).astype(BF16)


def prepare(tokens, routes, route_weights, exponents, arrays, experts):
    height = tokens.shape[0]
    side, width = min(arrays[0].shape), max(arrays[0].shape)
    per_block, blocks = side // LANES, width // side
    group = max(n for n in (1, 2, 4) if blocks % n == 0)
    groups = [(n, at) for n in range(len(arrays)) for at in range(0, blocks, group)]

    def kernel(exp_in, tokens_ref, routes_in, route_weights_ref, *refs):
        ins, refs = refs[: len(arrays)], refs[len(arrays) :]
        rows_out, out_ref, exp_ref, routes_ref, sems, small_sems = refs

        def copies(n, at):
            if ins[n].shape[0] == width:
                src = ins[n].at[pl.ds(at * side, group * side), :]
                dst = out_ref.at[pl.ds(n * width + at * side, group * side), :]
                return [pltpu.make_async_copy(src, dst, sems.at[n, at])]
            return [
                pltpu.make_async_copy(
                    ins[n].at[:, pl.ds(j * side, side)],
                    out_ref.at[pl.ds(n * width + j * side, side), :],
                    sems.at[n, j],
                )
                for j in range(at, at + group)
            ]

        def scale(n, at):
            tall = ins[n].shape[0] == width
            for j in range(at, at + group):
                for a in range(per_block):
                    for b in range(per_block):
                        along, across = (a, b) if tall else (b, a)
                        strip = j * per_block + along
                        exponent = exp_ref[n, across, strip]
                        factor = jnp.left_shift(1, exponent + 16).astype(F32) * 2.0**-16
                        row = n * width + j * side + a * LANES
                        place = (slice(row, row + LANES), slice(b * LANES, (b + 1) * LANES))
                        out_ref[place] = scaled(out_ref[place], factor)

        small = [
            pltpu.make_async_copy(exp_in, exp_ref, small_sems.at[0]),
            pltpu.make_async_copy(routes_in, routes_ref, small_sems.at[1]),
            pltpu.make_async_copy(tokens_ref, rows_out.at[:, pl.ds(0, width)], small_sems.at[2]),
        ]
        for copy in small:
            copy.start()
        for n in range(len(groups) + AHEAD):
            if n < len(groups):
                for copy in copies(*groups[n]):
                    copy.start()
            if n == AHEAD:
                for copy in small:
                    copy.wait()
                lane = lax.broadcasted_iota(jnp.int32, (LANES, height), 0)
                table = jnp.zeros((LANES, height), F32)
                for step in range(TICKS):
                    for k in range(routes.shape[1]):
                        named = routes_ref[step, k : k + 1, :] + step * experts
                        weight = route_weights_ref[step].astype(F32)[k : k + 1, :]
                        table += jnp.where(lane == named, weight, 0.0)
                rows_out[:, width:] = table.T.astype(BF16)
            if n >= AHEAD:
                for copy in copies(*groups[n - AHEAD]):
                    copy.wait()
                scale(*groups[n - AHEAD])

    vmem, hbm = (pl.BlockSpec(memory_space=space) for space in (pltpu.VMEM, pltpu.HBM))
    return pl.pallas_call(
        kernel,
        in_specs=[hbm, hbm, hbm, vmem] + [hbm] * len(arrays),
        out_specs=[vmem] * 2,
        out_shape=[
            jax.ShapeDtypeStruct((height, width + LANES), BF16),
            jax.ShapeDtypeStruct((len(arrays) * width, side), BF16),
        ],
        scratch_shapes=[
            pltpu.SMEM(exponents.shape, jnp.int32),
            pltpu.VMEM(routes.shape, jnp.int32),
            pltpu.SemaphoreType.DMA((len(arrays), blocks)),
            pltpu.SemaphoreType.DMA((3,)),
        ],
        compiler_params=pltpu.CompilerParams(vmem_limit_bytes=VMEM_LIMIT),
        cost_estimate=pl.CostEstimate(
            flops=len(arrays) * width * side,
            bytes_accessed=4 * len(arrays) * width * side,
            transcendentals=0,
        ),
        name="prepare",
    )(
        *(pltpu.with_memory_space_constraint(a, pltpu.HBM) for a in (exponents, tokens, routes)),
        route_weights,
        *(pltpu.with_memory_space_constraint(w, pltpu.HBM) for w in arrays),
    )


def experts_share(pieces, gain, weights, table, first_lane):
    width = gain.shape[1]
    side = weights[0].shape[1]
    height = pieces[0].shape[0]
    rows = 8 * height
    cut = cut_of(width)
    tile = side * max(n for n in (1, 2, 4) if width // side % n == 0)
    n_pieces = len(pieces)
    new_table = table is None

    def kernel(*refs):
        ins, gain_ref = refs[:n_pieces], refs[n_pieces]
        cores, rest = refs[n_pieces + 1 : n_pieces + 3], refs[n_pieces + 3 :]
        if not new_table:
            table_in, rest = rest[0], rest[1:]
        outs, table_ref = rest[:9], rest[9]
        rows_ref, squares_ref, hidden_ref = rest[10:]

        load_rows(ins, gain_ref, rows_ref, squares_ref)
        if new_table:
            load_table(ins, width, table_ref)
        else:
            table_ref[...] = table_in[...]
        mean = jnp.sum(squares_ref[...], axis=-1, keepdims=True) / width
        factor = lax.rsqrt(mean + 1e-06)
        lane = lax.broadcasted_iota(jnp.int32, (rows, LANES), 1)
        own_lane = first_lane + lax.div(lax.axis_index("expert"), SPLIT)
        picked = jnp.where(lane == own_lane, table_ref[...], 0.0)
        weight = jnp.sum(picked, axis=-1, keepdims=True)

        for core, ref in enumerate(cores):
            gate = jnp.dot(rows_ref[...], ref[:width, :], preferred_element_type=F32)
            up = jnp.dot(rows_ref[...], ref[width : 2 * width, :], preferred_element_type=F32)
            gate, up = gate * factor, up * factor
            hidden_ref[:, core * side : (core + 1) * side] = (
                gate / (1.0 + jnp.exp(-gate)) * up
            ).astype(BF16)

        for lo in range(0, width, side):
            product = sum(
                jnp.dot(
                    hidden_ref[:, core * side : (core + 1) * side],
                    ref[2 * width + lo : 2 * width + lo + side, :],
                    preferred_element_type=F32,
                )
                for core, ref in enumerate(cores)
            )
            product = product * weight
            hi = lo + side
            kept = ins[0][:, lo:hi].astype(F32) + product[:height, :]
            outs[0][:, lo:hi] = kept.astype(BF16)
            product = product.astype(BF16)
            for n in range(1, 7):
                outs[n][:, lo:hi] = product[n * height : (n + 1) * height, :]
            last = product[7 * height :, :]
            if lo < cut:
                outs[7][:, lo : min(hi, cut)] = last[:, : min(hi, cut) - lo]
            if hi > cut:
                outs[8][:, max(lo, cut) - cut : hi - cut] = last[:, max(lo, cut) - lo :]

    vmem = pl.BlockSpec(memory_space=pltpu.VMEM)
    tables = [] if new_table else [table]
    held = [pltpu.with_memory_space_constraint(w, pltpu.VMEM) for w in weights]
    operands = [*pieces, gain, *held, *tables]
    out_sizes = [(height, width)] * 7 + [(height, cut), (height, width - cut)]
    results = pl.pallas_call(
        kernel,
        in_specs=[vmem] * len(operands),
        out_specs=[vmem] * 10,
        out_shape=[jax.ShapeDtypeStruct(s, BF16) for s in out_sizes]
        + [jax.ShapeDtypeStruct((rows, LANES), F32)],
        scratch_shapes=[
            pltpu.VMEM((rows, width), BF16),
            pltpu.VMEM((rows, LANES), F32),
            pltpu.VMEM((rows, 2 * side), BF16),
        ],
        compiler_params=pltpu.CompilerParams(vmem_limit_bytes=VMEM_LIMIT),
        cost_estimate=pl.CostEstimate(
            flops=12 * rows * width * side,
            bytes_accessed=12 * width * side,
            transcendentals=2 * rows * side,
        ),
        name="experts_share",
    )(*operands)
    return results[:9], results[9]


def per_device(
    tokens, norm_gain, gate_weight, up_weight, down_weight, block_scales, routes, route_weights
):
    experts = lax.axis_size("expert") // SPLIT
    rows, own = prepare(
        tokens[0],
        routes[0].transpose(0, 2, 1),
        route_weights[0].transpose(0, 2, 1),
        block_scales[0].transpose(0, 2, 1),
        (gate_weight[0], up_weight[0], down_weight[0]),
        experts,
    )
    weights = (own, other_core(own))

    held_table = None
    for tick in range(TICKS):
        pieces = gather_second(gather_first(rows))
        outs, held_table = experts_share(
            pieces, norm_gain, weights, held_table, tick * experts
        )
        rows = sum_to_next(outs)
    return rows[None]


def solution(mesh):
    in_specs = (
        P("section", "expert", None),
        P("section", None),
        P("section", None, "expert"),
        P("section", None, "expert"),
        P("section", "expert", None),
        P("section", None, None, "expert"),
        P("section", None, "expert", None),
        P("section", None, "expert", None),
    )
    out_specs = P("section", "expert", None)
    return jax.shard_map(
        per_device, mesh=mesh, in_specs=in_specs, out_specs=out_specs, check_vma=False
    )
```

```python
import jax
import jax.numpy as jnp
from jax import lax
from jax.experimental import pallas as pl
from jax.experimental.pallas import tpu as pltpu
from jax.sharding import PartitionSpec as P

SPLIT = 4
TICKS = 2
LANES = 128
VMEM_LIMIT = 16 * 1024 * 1024
AHEAD = 10
F32 = jnp.float32
BF16 = jnp.bfloat16


def along_z(shard, by):
    length = lax.axis_size("expert")
    return lax.ppermute(
        shard, "expert", [(i, (i + 2 * by) % length) for i in range(length)]
    )


def other_core(shard):
    length = lax.axis_size("expert")
    return lax.ppermute(shard, "expert", [(i, i ^ 1) for i in range(length)])


def to_next_section(shard, by):
    sections, length = lax.axis_size("section"), lax.axis_size("expert")
    pairs = [
        (s * length + e, (s + 1) % sections * length + (e + 2 * by) % length)
        for s in range(sections)
        for e in range(length)
    ]
    return lax.ppermute(shard, ("section", "expert"), pairs)


def cut_of(width):
    return width // LANES // 2 * LANES


def gather(rows):
    back, ahead = rows, rows
    blocks = [rows]
    for _ in range(3):
        back, ahead = along_z(back, 1), along_z(ahead, -1)
        blocks += [back, ahead]
    cut = cut_of(rows.shape[1])
    return blocks + [along_z(back[:, :cut], 1), along_z(ahead[:, cut:], -1)]


def sum_to_next(outs):
    far = [
        along_z(outs[7], -2),
        along_z(outs[8], 2),
        along_z(outs[5], -1),
        along_z(outs[6], 1),
    ]
    far[0], near_back = lax.optimization_barrier((far[0], outs[1]))
    far[1], near_ahead = lax.optimization_barrier((far[1], outs[2]))
    near = [along_z(near_back, -1), along_z(near_ahead, 1)]
    back, ahead = join_far(outs[3], outs[4], *far)
    parts = [to_next_section(back, -2), to_next_section(ahead, 2)]
    parts.append(to_next_section(join_near(outs[0], *near), 0))
    return sum(part.astype(F32) for part in parts).astype(BF16)


def join_near(own, back, ahead):
    def kernel(own, back, ahead, out):
        f = lambda ref: ref[...].astype(F32)
        out[...] = (f(own) + (f(back) + f(ahead))).astype(BF16)

    return pl.pallas_call(
        kernel,
        out_shape=jax.ShapeDtypeStruct(own.shape, BF16),
        compiler_params=pltpu.CompilerParams(vmem_limit_bytes=VMEM_LIMIT),
        cost_estimate=pl.CostEstimate(
            flops=2 * own.size, bytes_accessed=8 * own.size, transcendentals=0
        ),
        name="join_near",
    )(own, back, ahead)


def join_far(back, ahead, left, right, back_3, ahead_3):
    width = back.shape[1]
    cut = cut_of(width)

    def kernel(back, ahead, left, right, b3, a3, back_out, ahead_out):
        lo, hi = slice(0, cut), slice(cut, width)
        f = lambda ref, cols: ref[:, cols].astype(F32)
        back_out[:, lo] = (f(back, lo) + f(b3, lo) + left[...].astype(F32)).astype(BF16)
        back_out[:, hi] = (f(back, hi) + f(b3, hi)).astype(BF16)
        ahead_out[:, lo] = (f(ahead, lo) + f(a3, lo)).astype(BF16)
        ahead_out[:, hi] = (f(ahead, hi) + f(a3, hi) + right[...].astype(F32)).astype(BF16)

    rows = back.shape[0]
    return pl.pallas_call(
        kernel,
        out_shape=[jax.ShapeDtypeStruct((rows, width), BF16)] * 2,
        compiler_params=pltpu.CompilerParams(vmem_limit_bytes=VMEM_LIMIT),
        cost_estimate=pl.CostEstimate(
            flops=6 * rows * width, bytes_accessed=14 * rows * width, transcendentals=0
        ),
        name="join_far",
    )(back, ahead, left, right, back_3, ahead_3)


def load_rows(pieces, gain, rows_ref, squares_ref):
    height = pieces[0].shape[0]
    width = gain.shape[1]
    cut = cut_of(pieces[0].shape[1])

    def put(ref, at, lo, hi, base):
        held = None
        for c in range(lo, hi, LANES):
            x = ref[:, c - base : c - base + LANES].astype(F32)
            held = x * x if held is None else held + x * x
            rows_ref[at : at + height, c : c + LANES] = (
                x * gain[:, c : c + LANES]
            ).astype(BF16)
        return held

    for n in range(8):
        at = n * height
        if n < 7:
            held = put(pieces[n], at, 0, width, 0)
        else:
            held = put(pieces[7], at, 0, cut, 0) + put(pieces[8], at, cut, width, cut)
        squares_ref[at : at + height, :] = held


def load_table(pieces, width, table_ref):
    height = pieces[0].shape[0]
    cut = cut_of(pieces[0].shape[1])
    for n in range(8):
        ref, lo = (pieces[n], width) if n < 7 else (pieces[8], width - cut)
        table_ref[n * height : (n + 1) * height, :] = ref[:, lo : lo + LANES].astype(F32)


def scaled(block, factor):
    return block * jnp.full(block.shape, factor, F32).astype(BF16)


def prepare(tokens, routes, route_weights, exponents, arrays, experts):
    height = tokens.shape[0]
    side, width = min(arrays[0].shape), max(arrays[0].shape)
    per_block, blocks = side // LANES, width // side
    group = max(n for n in (1, 2, 4) if blocks % n == 0)
    groups = [(n, at) for n in range(len(arrays)) for at in range(0, blocks, group)]

    def kernel(exp_in, tokens_ref, routes_in, route_weights_ref, *refs):
        ins, refs = refs[: len(arrays)], refs[len(arrays) :]
        rows_out, out_ref, exp_ref, routes_ref, sems, small_sems = refs

        def copies(n, at):
            if ins[n].shape[0] == width:
                src = ins[n].at[pl.ds(at * side, group * side), :]
                dst = out_ref.at[pl.ds(n * width + at * side, group * side), :]
                return [pltpu.make_async_copy(src, dst, sems.at[n, at])]
            return [
                pltpu.make_async_copy(
                    ins[n].at[:, pl.ds(j * side, side)],
                    out_ref.at[pl.ds(n * width + j * side, side), :],
                    sems.at[n, j],
                )
                for j in range(at, at + group)
            ]

        def scale(n, at):
            tall = ins[n].shape[0] == width
            for j in range(at, at + group):
                for a in range(per_block):
                    for b in range(per_block):
                        along, across = (a, b) if tall else (b, a)
                        strip = j * per_block + along
                        exponent = exp_ref[n, across, strip]
                        factor = jnp.left_shift(1, exponent + 16).astype(F32) * 2.0**-16
                        row = n * width + j * side + a * LANES
                        place = (slice(row, row + LANES), slice(b * LANES, (b + 1) * LANES))
                        out_ref[place] = scaled(out_ref[place], factor)

        small = [
            pltpu.make_async_copy(exp_in, exp_ref, small_sems.at[0]),
            pltpu.make_async_copy(routes_in, routes_ref, small_sems.at[1]),
            pltpu.make_async_copy(tokens_ref, rows_out.at[:, pl.ds(0, width)], small_sems.at[2]),
        ]
        for copy in small:
            copy.start()
        for n in range(len(groups) + AHEAD):
            if n < len(groups):
                for copy in copies(*groups[n]):
                    copy.start()
            if n == AHEAD:
                for copy in small:
                    copy.wait()
                lane = lax.broadcasted_iota(jnp.int32, (LANES, height), 0)
                table = jnp.zeros((LANES, height), F32)
                for step in range(TICKS):
                    for k in range(routes.shape[1]):
                        named = routes_ref[step, k : k + 1, :] + step * experts
                        weight = route_weights_ref[step].astype(F32)[k : k + 1, :]
                        table += jnp.where(lane == named, weight, 0.0)
                rows_out[:, width:] = table.T.astype(BF16)
            if n >= AHEAD:
                for copy in copies(*groups[n - AHEAD]):
                    copy.wait()
                scale(*groups[n - AHEAD])

    vmem, hbm = (pl.BlockSpec(memory_space=space) for space in (pltpu.VMEM, pltpu.HBM))
    return pl.pallas_call(
        kernel,
        in_specs=[hbm, hbm, hbm, vmem] + [hbm] * len(arrays),
        out_specs=[vmem] * 2,
        out_shape=[
            jax.ShapeDtypeStruct((height, width + LANES), BF16),
            jax.ShapeDtypeStruct((len(arrays) * width, side), BF16),
        ],
        scratch_shapes=[
            pltpu.SMEM(exponents.shape, jnp.int32),
            pltpu.VMEM(routes.shape, jnp.int32),
            pltpu.SemaphoreType.DMA((len(arrays), blocks)),
            pltpu.SemaphoreType.DMA((3,)),
        ],
        compiler_params=pltpu.CompilerParams(vmem_limit_bytes=VMEM_LIMIT),
        cost_estimate=pl.CostEstimate(
            flops=len(arrays) * width * side,
            bytes_accessed=4 * len(arrays) * width * side,
            transcendentals=0,
        ),
        name="prepare",
    )(
        *(pltpu.with_memory_space_constraint(a, pltpu.HBM) for a in (exponents, tokens, routes)),
        route_weights,
        *(pltpu.with_memory_space_constraint(w, pltpu.HBM) for w in arrays),
    )


def experts_share(pieces, gain, weights, table, first_lane):
    width = gain.shape[1]
    side = weights[0].shape[1]
    height = pieces[0].shape[0]
    rows = 8 * height
    cut = cut_of(width)
    tile = side * max(n for n in (1, 2, 4) if width // side % n == 0)
    n_pieces = len(pieces)
    new_table = table is None

    def kernel(*refs):
        ins, gain_ref = refs[:n_pieces], refs[n_pieces]
        cores, rest = refs[n_pieces + 1 : n_pieces + 3], refs[n_pieces + 3 :]
        if not new_table:
            table_in, rest = rest[0], rest[1:]
        outs, table_ref = rest[:9], rest[9]
        rows_ref, squares_ref, hidden_ref = rest[10:]

        load_rows(ins, gain_ref, rows_ref, squares_ref)
        if new_table:
            load_table(ins, width, table_ref)
        else:
            table_ref[...] = table_in[...]
        mean = jnp.sum(squares_ref[...], axis=-1, keepdims=True) / width
        factor = lax.rsqrt(mean + 1e-06)
        lane = lax.broadcasted_iota(jnp.int32, (rows, LANES), 1)
        own_lane = first_lane + lax.div(lax.axis_index("expert"), SPLIT)
        picked = jnp.where(lane == own_lane, table_ref[...], 0.0)
        weight = jnp.sum(picked, axis=-1, keepdims=True)

        for core, ref in enumerate(cores):
            gate = jnp.dot(rows_ref[...], ref[:width, :], preferred_element_type=F32)
            up = jnp.dot(rows_ref[...], ref[width : 2 * width, :], preferred_element_type=F32)
            gate, up = gate * factor, up * factor
            hidden_ref[:, core * side : (core + 1) * side] = (
                gate / (1.0 + jnp.exp(-gate)) * up
            ).astype(BF16)

        for lo in range(0, width, side):
            product = sum(
                jnp.dot(
                    hidden_ref[:, core * side : (core + 1) * side],
                    ref[2 * width + lo : 2 * width + lo + side, :],
                    preferred_element_type=F32,
                )
                for core, ref in enumerate(cores)
            )
            product = product * weight
            hi = lo + side
            kept = ins[0][:, lo:hi].astype(F32) + product[:height, :]
            outs[0][:, lo:hi] = kept.astype(BF16)
            product = product.astype(BF16)
            for n in range(1, 7):
                outs[n][:, lo:hi] = product[n * height : (n + 1) * height, :]
            last = product[7 * height :, :]
            if lo < cut:
                outs[7][:, lo : min(hi, cut)] = last[:, : min(hi, cut) - lo]
            if hi > cut:
                outs[8][:, max(lo, cut) - cut : hi - cut] = last[:, max(lo, cut) - lo :]

    vmem = pl.BlockSpec(memory_space=pltpu.VMEM)
    tables = [] if new_table else [table]
    held = [pltpu.with_memory_space_constraint(w, pltpu.VMEM) for w in weights]
    operands = [*pieces, gain, *held, *tables]
    out_sizes = [(height, width)] * 7 + [(height, cut), (height, width - cut)]
    results = pl.pallas_call(
        kernel,
        in_specs=[vmem] * len(operands),
        out_specs=[vmem] * 10,
        out_shape=[jax.ShapeDtypeStruct(s, BF16) for s in out_sizes]
        + [jax.ShapeDtypeStruct((rows, LANES), F32)],
        scratch_shapes=[
            pltpu.VMEM((rows, width), BF16),
            pltpu.VMEM((rows, LANES), F32),
            pltpu.VMEM((rows, 2 * side), BF16),
        ],
        compiler_params=pltpu.CompilerParams(vmem_limit_bytes=VMEM_LIMIT),
        cost_estimate=pl.CostEstimate(
            flops=12 * rows * width * side,
            bytes_accessed=12 * width * side,
            transcendentals=2 * rows * side,
        ),
        name="experts_share",
    )(*operands)
    return results[:9], results[9]


def per_device(
    tokens, norm_gain, gate_weight, up_weight, down_weight, block_scales, routes, route_weights
):
    experts = lax.axis_size("expert") // SPLIT
    rows, own = prepare(
        tokens[0],
        routes[0].transpose(0, 2, 1),
        route_weights[0].transpose(0, 2, 1),
        block_scales[0].transpose(0, 2, 1),
        (gate_weight[0], up_weight[0], down_weight[0]),
        experts,
    )
    weights = (own, other_core(own))

    held_table = None
    for tick in range(TICKS):
        pieces = gather(rows)
        outs, held_table = experts_share(
            pieces, norm_gain, weights, held_table, tick * experts
        )
        rows = sum_to_next(outs)
    return rows[None]


def solution(mesh):
    in_specs = (
        P("section", "expert", None),
        P("section", None),
        P("section", None, "expert"),
        P("section", None, "expert"),
        P("section", "expert", None),
        P("section", None, None, "expert"),
        P("section", None, "expert", None),
        P("section", None, "expert", None),
    )
    out_specs = P("section", "expert", None)
    return jax.shard_map(
        per_device, mesh=mesh, in_specs=in_specs, out_specs=out_specs, check_vma=False
    )
```

```python
import jax
import jax.numpy as jnp
from jax import lax
from jax.experimental import pallas as pl
from jax.experimental.pallas import tpu as pltpu
from jax.sharding import PartitionSpec as P

SPLIT = 4
TICKS = 2
LANES = 128
VMEM_LIMIT = 16 * 1024 * 1024
AHEAD = 10
F32 = jnp.float32
BF16 = jnp.bfloat16


def z_places(place, by):
    return 2 * by if place % 2 == 0 else -2 * by


def along_z(shard, by):
    length = lax.axis_size("expert")
    return lax.ppermute(
        shard, "expert", [(i, (i + z_places(i, by)) % length) for i in range(length)]
    )


def other_core(shard):
    length = lax.axis_size("expert")
    return lax.ppermute(shard, "expert", [(i, i ^ 1) for i in range(length)])


def to_next_section(shard, by):
    sections, length = lax.axis_size("section"), lax.axis_size("expert")
    pairs = [
        (s * length + e, (s + 1) % sections * length + (e + z_places(e, by)) % length)
        for s in range(sections)
        for e in range(length)
    ]
    return lax.ppermute(shard, ("section", "expert"), pairs)


def cut_of(width):
    return width // LANES // 2 * LANES


def gather(rows):
    back, ahead = rows, rows
    blocks = [rows]
    for _ in range(3):
        back, ahead = along_z(back, 1), along_z(ahead, -1)
        blocks += [back, ahead]
    cut = cut_of(rows.shape[1])
    return blocks + [along_z(back[:, :cut], 1), along_z(ahead[:, cut:], -1)]


def sum_to_next(outs):
    far = [
        along_z(outs[7], -2),
        along_z(outs[8], 2),
        along_z(outs[5], -1),
        along_z(outs[6], 1),
    ]
    far[0], near_back = lax.optimization_barrier((far[0], outs[1]))
    far[1], near_ahead = lax.optimization_barrier((far[1], outs[2]))
    near = [along_z(near_back, -1), along_z(near_ahead, 1)]
    back, ahead = join_far(outs[3], outs[4], *far)
    parts = [to_next_section(back, -2), to_next_section(ahead, 2)]
    parts.append(to_next_section(join_near(outs[0], *near), 0))
    return sum(part.astype(F32) for part in parts).astype(BF16)


def join_near(own, back, ahead):
    def kernel(own, back, ahead, out):
        f = lambda ref: ref[...].astype(F32)
        out[...] = (f(own) + (f(back) + f(ahead))).astype(BF16)

    return pl.pallas_call(
        kernel,
        out_shape=jax.ShapeDtypeStruct(own.shape, BF16),
        compiler_params=pltpu.CompilerParams(vmem_limit_bytes=VMEM_LIMIT),
        cost_estimate=pl.CostEstimate(
            flops=2 * own.size, bytes_accessed=8 * own.size, transcendentals=0
        ),
        name="join_near",
    )(own, back, ahead)


def join_far(back, ahead, left, right, back_3, ahead_3):
    width = back.shape[1]
    cut = cut_of(width)

    def kernel(back, ahead, left, right, b3, a3, back_out, ahead_out):
        lo, hi = slice(0, cut), slice(cut, width)
        f = lambda ref, cols: ref[:, cols].astype(F32)
        back_out[:, lo] = (f(back, lo) + f(b3, lo) + left[...].astype(F32)).astype(BF16)
        back_out[:, hi] = (f(back, hi) + f(b3, hi)).astype(BF16)
        ahead_out[:, lo] = (f(ahead, lo) + f(a3, lo)).astype(BF16)
        ahead_out[:, hi] = (f(ahead, hi) + f(a3, hi) + right[...].astype(F32)).astype(BF16)

    rows = back.shape[0]
    return pl.pallas_call(
        kernel,
        out_shape=[jax.ShapeDtypeStruct((rows, width), BF16)] * 2,
        compiler_params=pltpu.CompilerParams(vmem_limit_bytes=VMEM_LIMIT),
        cost_estimate=pl.CostEstimate(
            flops=6 * rows * width, bytes_accessed=14 * rows * width, transcendentals=0
        ),
        name="join_far",
    )(back, ahead, left, right, back_3, ahead_3)


def load_rows(pieces, gain, rows_ref, squares_ref):
    height = pieces[0].shape[0]
    width = gain.shape[1]
    cut = cut_of(pieces[0].shape[1])

    def put(ref, at, lo, hi, base):
        held = None
        for c in range(lo, hi, LANES):
            x = ref[:, c - base : c - base + LANES].astype(F32)
            held = x * x if held is None else held + x * x
            rows_ref[at : at + height, c : c + LANES] = (
                x * gain[:, c : c + LANES]
            ).astype(BF16)
        return held

    for n in range(8):
        at = n * height
        if n < 7:
            held = put(pieces[n], at, 0, width, 0)
        else:
            held = put(pieces[7], at, 0, cut, 0) + put(pieces[8], at, cut, width, cut)
        squares_ref[at : at + height, :] = held


def load_table(pieces, width, table_ref):
    height = pieces[0].shape[0]
    cut = cut_of(pieces[0].shape[1])
    for n in range(8):
        ref, lo = (pieces[n], width) if n < 7 else (pieces[8], width - cut)
        table_ref[n * height : (n + 1) * height, :] = ref[:, lo : lo + LANES].astype(F32)


def scaled(block, factor):
    return block * jnp.full(block.shape, factor, F32).astype(BF16)


def prepare(tokens, routes, route_weights, exponents, arrays, experts):
    height = tokens.shape[0]
    side, width = min(arrays[0].shape), max(arrays[0].shape)
    per_block, blocks = side // LANES, width // side
    group = max(n for n in (1, 2, 4) if blocks % n == 0)
    groups = [(n, at) for n in range(len(arrays)) for at in range(0, blocks, group)]

    def kernel(exp_in, tokens_ref, routes_in, route_weights_ref, *refs):
        ins, refs = refs[: len(arrays)], refs[len(arrays) :]
        rows_out, out_ref, exp_ref, routes_ref, sems, small_sems = refs

        def copies(n, at):
            if ins[n].shape[0] == width:
                src = ins[n].at[pl.ds(at * side, group * side), :]
                dst = out_ref.at[pl.ds(n * width + at * side, group * side), :]
                return [pltpu.make_async_copy(src, dst, sems.at[n, at])]
            return [
                pltpu.make_async_copy(
                    ins[n].at[:, pl.ds(j * side, side)],
                    out_ref.at[pl.ds(n * width + j * side, side), :],
                    sems.at[n, j],
                )
                for j in range(at, at + group)
            ]

        def scale(n, at):
            tall = ins[n].shape[0] == width
            for j in range(at, at + group):
                for a in range(per_block):
                    for b in range(per_block):
                        along, across = (a, b) if tall else (b, a)
                        strip = j * per_block + along
                        exponent = exp_ref[n, across, strip]
                        factor = jnp.left_shift(1, exponent + 16).astype(F32) * 2.0**-16
                        row = n * width + j * side + a * LANES
                        place = (slice(row, row + LANES), slice(b * LANES, (b + 1) * LANES))
                        out_ref[place] = scaled(out_ref[place], factor)

        small = [
            pltpu.make_async_copy(exp_in, exp_ref, small_sems.at[0]),
            pltpu.make_async_copy(routes_in, routes_ref, small_sems.at[1]),
            pltpu.make_async_copy(tokens_ref, rows_out.at[:, pl.ds(0, width)], small_sems.at[2]),
        ]
        for copy in small:
            copy.start()
        for n in range(len(groups) + AHEAD):
            if n < len(groups):
                for copy in copies(*groups[n]):
                    copy.start()
            if n == AHEAD:
                for copy in small:
                    copy.wait()
                lane = lax.broadcasted_iota(jnp.int32, (LANES, height), 0)
                table = jnp.zeros((LANES, height), F32)
                for step in range(TICKS):
                    for k in range(routes.shape[1]):
                        named = routes_ref[step, k : k + 1, :] + step * experts
                        weight = route_weights_ref[step].astype(F32)[k : k + 1, :]
                        table += jnp.where(lane == named, weight, 0.0)
                rows_out[:, width:] = table.T.astype(BF16)
            if n >= AHEAD:
                for copy in copies(*groups[n - AHEAD]):
                    copy.wait()
                scale(*groups[n - AHEAD])

    vmem, hbm = (pl.BlockSpec(memory_space=space) for space in (pltpu.VMEM, pltpu.HBM))
    return pl.pallas_call(
        kernel,
        in_specs=[hbm, hbm, hbm, vmem] + [hbm] * len(arrays),
        out_specs=[vmem] * 2,
        out_shape=[
            jax.ShapeDtypeStruct((height, width + LANES), BF16),
            jax.ShapeDtypeStruct((len(arrays) * width, side), BF16),
        ],
        scratch_shapes=[
            pltpu.SMEM(exponents.shape, jnp.int32),
            pltpu.VMEM(routes.shape, jnp.int32),
            pltpu.SemaphoreType.DMA((len(arrays), blocks)),
            pltpu.SemaphoreType.DMA((3,)),
        ],
        compiler_params=pltpu.CompilerParams(vmem_limit_bytes=VMEM_LIMIT),
        cost_estimate=pl.CostEstimate(
            flops=len(arrays) * width * side,
            bytes_accessed=4 * len(arrays) * width * side,
            transcendentals=0,
        ),
        name="prepare",
    )(
        *(pltpu.with_memory_space_constraint(a, pltpu.HBM) for a in (exponents, tokens, routes)),
        route_weights,
        *(pltpu.with_memory_space_constraint(w, pltpu.HBM) for w in arrays),
    )


def experts_share(pieces, gain, weights, table, first_lane):
    width = gain.shape[1]
    side = weights[0].shape[1]
    height = pieces[0].shape[0]
    rows = 8 * height
    cut = cut_of(width)
    tile = side * max(n for n in (1, 2, 4) if width // side % n == 0)
    n_pieces = len(pieces)
    new_table = table is None

    def kernel(*refs):
        ins, gain_ref = refs[:n_pieces], refs[n_pieces]
        cores, rest = refs[n_pieces + 1 : n_pieces + 3], refs[n_pieces + 3 :]
        if not new_table:
            table_in, rest = rest[0], rest[1:]
        outs, table_ref = rest[:9], rest[9]
        rows_ref, squares_ref, hidden_ref = rest[10:]

        load_rows(ins, gain_ref, rows_ref, squares_ref)
        if new_table:
            load_table(ins, width, table_ref)
        else:
            table_ref[...] = table_in[...]
        mean = jnp.sum(squares_ref[...], axis=-1, keepdims=True) / width
        factor = lax.rsqrt(mean + 1e-06)
        lane = lax.broadcasted_iota(jnp.int32, (rows, LANES), 1)
        own_lane = first_lane + lax.div(lax.axis_index("expert"), SPLIT)
        picked = jnp.where(lane == own_lane, table_ref[...], 0.0)
        weight = jnp.sum(picked, axis=-1, keepdims=True)

        for core, ref in enumerate(cores):
            gate = jnp.dot(rows_ref[...], ref[:width, :], preferred_element_type=F32)
            up = jnp.dot(rows_ref[...], ref[width : 2 * width, :], preferred_element_type=F32)
            gate, up = gate * factor, up * factor
            hidden_ref[:, core * side : (core + 1) * side] = (
                gate / (1.0 + jnp.exp(-gate)) * up
            ).astype(BF16)

        for lo in range(0, width, side):
            product = sum(
                jnp.dot(
                    hidden_ref[:, core * side : (core + 1) * side],
                    ref[2 * width + lo : 2 * width + lo + side, :],
                    preferred_element_type=F32,
                )
                for core, ref in enumerate(cores)
            )
            product = product * weight
            hi = lo + side
            kept = ins[0][:, lo:hi].astype(F32) + product[:height, :]
            outs[0][:, lo:hi] = kept.astype(BF16)
            product = product.astype(BF16)
            for n in range(1, 7):
                outs[n][:, lo:hi] = product[n * height : (n + 1) * height, :]
            last = product[7 * height :, :]
            if lo < cut:
                outs[7][:, lo : min(hi, cut)] = last[:, : min(hi, cut) - lo]
            if hi > cut:
                outs[8][:, max(lo, cut) - cut : hi - cut] = last[:, max(lo, cut) - lo :]

    vmem = pl.BlockSpec(memory_space=pltpu.VMEM)
    tables = [] if new_table else [table]
    held = [pltpu.with_memory_space_constraint(w, pltpu.VMEM) for w in weights]
    operands = [*pieces, gain, *held, *tables]
    out_sizes = [(height, width)] * 7 + [(height, cut), (height, width - cut)]
    results = pl.pallas_call(
        kernel,
        in_specs=[vmem] * len(operands),
        out_specs=[vmem] * 10,
        out_shape=[jax.ShapeDtypeStruct(s, BF16) for s in out_sizes]
        + [jax.ShapeDtypeStruct((rows, LANES), F32)],
        scratch_shapes=[
            pltpu.VMEM((rows, width), BF16),
            pltpu.VMEM((rows, LANES), F32),
            pltpu.VMEM((rows, 2 * side), BF16),
        ],
        compiler_params=pltpu.CompilerParams(vmem_limit_bytes=VMEM_LIMIT),
        cost_estimate=pl.CostEstimate(
            flops=12 * rows * width * side,
            bytes_accessed=12 * width * side,
            transcendentals=2 * rows * side,
        ),
        name="experts_share",
    )(*operands)
    return results[:9], results[9]


def per_device(
    tokens, norm_gain, gate_weight, up_weight, down_weight, block_scales, routes, route_weights
):
    experts = lax.axis_size("expert") // SPLIT
    rows, own = prepare(
        tokens[0],
        routes[0].transpose(0, 2, 1),
        route_weights[0].transpose(0, 2, 1),
        block_scales[0].transpose(0, 2, 1),
        (gate_weight[0], up_weight[0], down_weight[0]),
        experts,
    )
    weights = (own, other_core(own))

    held_table = None
    for tick in range(TICKS):
        pieces = gather(rows)
        outs, held_table = experts_share(
            pieces, norm_gain, weights, held_table, tick * experts
        )
        rows = sum_to_next(outs)
    return rows[None]


def solution(mesh):
    in_specs = (
        P("section", "expert", None),
        P("section", None),
        P("section", None, "expert"),
        P("section", None, "expert"),
        P("section", "expert", None),
        P("section", None, None, "expert"),
        P("section", None, "expert", None),
        P("section", None, "expert", None),
    )
    out_specs = P("section", "expert", None)
    return jax.shard_map(
        per_device, mesh=mesh, in_specs=in_specs, out_specs=out_specs, check_vma=False
    )
```
